128 devices in a mesh: grp: 4 (over z_hi, core), leaf: 32 (over z_lo, y, x).
Axes of the slice: x: 4, y: 4, z: 4 (z_hi: 2, z_lo: 2; z = z_hi * 2 + z_lo), core: 2. Of those that a mesh axis runs over, the one named last changes fastest.
Arguments:
- features: float32 [131072, 128], P(('grp', 'leaf')), may hold values from -6 to 6
- tree_order: int32 [128, 1024], P(('grp', 'leaf')), may hold values from 0 to 1023, each once within a row
- gain_leaf: float32 [128], replicated, may hold values from 0.1 to 1.9
- w_qkv_leaf: float32 [128, 384], replicated
- w_out_leaf: float32 [128, 128], replicated, may hold values from -0.5 to 0.5
- w_pool1: float32 [512, 256], replicated, may hold values from -0.5 to 0.5
- w_pool2: float32 [1024, 384], replicated, may hold values from -0.375 to 0.375
- w_pool3: float32 [1536, 512], replicated, may hold values from -0.21875 to 0.21875
- gain_coarse: float32 [512], replicated, may hold values from 0.1 to 1.9
- w_query: float32 [512, 512], replicated
- w_keyval: float32 [512, 1024], replicated
- w_out: float32 [512, 512], replicated, may hold values from -0.25 to 0.25
- cotangent: float32 [2048, 512], P(('grp', 'leaf')), may hold values from -6 to 6
Outputs:
- output: float32 [2048, 512], P(('grp', 'leaf'))
- grad_gain_leaf: float32 [128], replicated
- grad_qkv_leaf: float32 [128, 384], replicated
- grad_out_leaf: float32 [128, 128], replicated
- grad_pool1: float32 [512, 256], replicated
- grad_pool2: float32 [1024, 384], replicated
- grad_pool3: float32 [1536, 512], replicated
- grad_gain_coarse: float32 [512], replicated
- grad_query: float32 [512, 512], replicated
- grad_keyval: float32 [512, 1024], replicated
- grad_out: float32 [512, 512], replicated
The draws below stay inside these ranges and needn't reach their ends.
Inputs may be any that keep to these rules, and one draw needn't show every extreme that they name: `tree_order`: each row lists the 1024 particles of one device, each once.
All inputs are finite; a program needn't handle non-finite values.
Results may differ from the reference program's by a relative error of at most 0.0003.
Values sent between devices are 32-bit elements; how exact they have to be, the bound alone decides.
No kernel may reach another device: no remote copies, remote signals or barrier semaphores. Data moves between devices by JAX's collectives and lax.ppermute only.
A program may use at most 128 MiB of HBM per device.

```python
import jax
import jax.numpy as jnp
from jax import lax

C_LEAF = 128
C_MID1 = 256
C_MID2 = 384
C_COARSE = 512
HEAD = 32
BALL = 128
ROOT_DEV = 2
POINTS_DEV = 1024
POINTS = 131072
COARSE_ROWS = 2048
N_GRP = 4
N_LEAF = 32


def draw_w_qkv_leaf(key, part):
    key = jax.random.fold_in(key, 11)
    matrix = jax.random.normal(key, (C_LEAF, 3 * C_LEAF), jnp.float32) * C_LEAF ** (-0.5)
    return matrix


def draw_w_query(key, part):
    key = jax.random.fold_in(key, 12)
    matrix = jax.random.normal(key, (C_COARSE, C_COARSE), jnp.float32) * C_COARSE ** (-0.5)
    return matrix


def draw_w_keyval(key, part):
    key = jax.random.fold_in(key, 13)
    matrix = jax.random.normal(key, (C_COARSE, 2 * C_COARSE), jnp.float32) * C_COARSE ** (-0.5)
    return matrix


def block_scale(rng, dims, pieces, least, high):
    level, own = 1.0, jax.random.fold_in(rng, 6)
    for axis_at, parts in pieces:
        steps = jnp.exp(jax.random.uniform(jax.random.fold_in(own, axis_at), (parts,), jnp.float32, least / len(pieces), high / len(pieces)))
        level = level * jnp.repeat(steps, dims[axis_at] // parts).reshape([-1 if axis == axis_at else 1 for axis in range(len(dims))])
    return level


def bell_draw(stream_key, shape, spread, limit, pieces=(), kind=jnp.bfloat16):
    drawn = spread * jax.random.normal(stream_key, shape, jnp.float32)
    if pieces:
        drawn = drawn * block_scale(stream_key, shape, pieces, -0.22, 0.18)
    return jnp.clip(drawn, -limit, limit).astype(kind)


def setup_inputs(seed: int = 0) -> dict:
    key_of = jax.random.split(jax.random.key(seed), 14)
    return {
        "features": bell_draw(key_of[0], (POINTS, C_LEAF), 1.0, 6.0, ((0, 128),), jnp.float32),
        "tree_order": jax.vmap(lambda own: jax.random.permutation(own, POINTS_DEV))(jax.random.split(key_of[1], (N_GRP * N_LEAF))).reshape((N_GRP * N_LEAF, POINTS_DEV)).astype(jnp.int32),
        "gain_leaf": jnp.clip(1.0 + 0.18 * jax.random.normal(key_of[2], (C_LEAF,), jnp.float32), 0.1, 1.9),
        "w_qkv_leaf": draw_w_qkv_leaf(jax.random.fold_in(key_of[13], 71), 0),
        "w_out_leaf": bell_draw(key_of[4], (C_LEAF, C_LEAF), C_LEAF ** -0.5, 0.5, (), jnp.float32),
        "w_pool1": bell_draw(key_of[5], (4 * C_LEAF, C_MID1), C_LEAF ** -0.5, 0.5, (), jnp.float32),
        "w_pool2": bell_draw(key_of[6], (4 * C_MID1, C_MID2), C_MID1 ** -0.5, 0.375, (), jnp.float32),
        "w_pool3": bell_draw(key_of[7], (4 * C_MID2, C_COARSE), (2 * C_MID2) ** -0.5, 0.21875, (), jnp.float32),
        "gain_coarse": jnp.clip(1.0 + 0.18 * jax.random.normal(key_of[8], (C_COARSE,), jnp.float32), 0.1, 1.9),
        "w_query": draw_w_query(jax.random.fold_in(key_of[13], 71), 0),
        "w_keyval": draw_w_keyval(jax.random.fold_in(key_of[13], 71), 0),
        "w_out": bell_draw(key_of[11], (C_COARSE, C_COARSE), C_COARSE ** -0.5, 0.25, (), jnp.float32),
        "cotangent": bell_draw(key_of[12], (COARSE_ROWS, C_COARSE), 1.0, 6.0, ((0, 128),), jnp.float32),
    }


MATMUL_ACCURACY = lax.Precision.HIGHEST

def matmul_high(left, right):
    return jnp.dot(left, right, precision=MATMUL_ACCURACY, preferred_element_type=jnp.float32)

def rms_scale(values, gain):
    return values * lax.rsqrt(lax.optimization_barrier(jnp.mean(values * values, axis=-1, keepdims=True)) + 1e-06) * gain

def leaf_front(ordered, gain_leaf, w_qkv_leaf, w_out_leaf, w_pool1, w_pool2, w_pool3):
    row_count, feature_width = ordered.shape
    head_count = feature_width // HEAD
    leaf_normed = rms_scale(ordered, gain_leaf)
    packed = matmul_high(leaf_normed, w_qkv_leaf).reshape(row_count // BALL, BALL, 3, head_count, HEAD)
    queries = packed[:, :, 0] * HEAD ** (-0.5)
    logit_scores = jnp.einsum('bihd,bjhd->bhij', queries, packed[:, :, 1], precision=MATMUL_ACCURACY)
    attention_weights = jax.nn.softmax(logit_scores, axis=-1)
    attended = jnp.einsum('bhij,bjhd->bihd', attention_weights, packed[:, :, 2], precision=MATMUL_ACCURACY)
    leaf_mixed = ordered + matmul_high(attended.reshape(row_count, feature_width), w_out_leaf)
    level_one = jax.nn.silu(matmul_high(leaf_mixed.reshape(row_count // 4, -1), w_pool1))
    level_two = jax.nn.silu(matmul_high(level_one.reshape(row_count // 16, -1), w_pool2))
    return matmul_high(level_two.reshape(row_count // 64, -1), w_pool3)

def summarize(coarse, gain_coarse):
    coarse_normed = rms_scale(coarse, gain_coarse)
    block_means = lax.optimization_barrier(jnp.mean(coarse.reshape(ROOT_DEV, -1, coarse.shape[-1]), axis=1))
    return (coarse_normed, rms_scale(block_means, gain_coarse))

def attend_part(queries, keyval):
    query_total, feature_width = queries.shape
    key_count = keyval.shape[0]
    head_count = feature_width // HEAD
    scaled_scores = queries.reshape(query_total, head_count, HEAD) * HEAD ** (-0.5)
    key_slice = keyval[:, :feature_width].reshape(key_count, head_count, HEAD)
    value_slice = keyval[:, feature_width:].reshape(key_count, head_count, HEAD)
    logit_scores = jnp.einsum('kzo,czo->zkc', scaled_scores, key_slice, precision=MATMUL_ACCURACY)
    attention_weights = jax.nn.softmax(logit_scores, axis=-1)
    return jnp.einsum('lut,tlk->ulk', attention_weights, value_slice, precision=MATMUL_ACCURACY).reshape(query_total, feature_width)

def attend(queries, group_keyval, root_keyval):
    return attend_part(queries, group_keyval) + attend_part(queries, root_keyval)

def reference(features, tree_order, gain_leaf, w_qkv_leaf, w_out_leaf, w_pool1, w_pool2, w_pool3, gain_coarse, w_query, w_keyval, w_out, cotangent):
    point_blocks = features.reshape(N_GRP * N_LEAF, POINTS_DEV, C_LEAF)

    def forward(weight_set):
        leaf_weights = weight_set[:6]

        def one_device(device_item):
            return leaf_front(device_item[0][device_item[1]], *leaf_weights)
        coarse = lax.map(jax.checkpoint(one_device), (point_blocks, tree_order))
        coarse_normed, root_rows = jax.vmap(summarize, in_axes=(0, None))(coarse, weight_set[6])
        flat_normed = coarse_normed.reshape(-1, C_COARSE)
        queries = matmul_high(flat_normed, weight_set[7]).reshape(N_GRP, -1, C_COARSE)
        group_keyval = matmul_high(flat_normed, weight_set[8]).reshape(N_GRP, -1, 2 * C_COARSE)
        root_keyval = matmul_high(root_rows.reshape(-1, C_COARSE), weight_set[8])

        def one_group(group_item):
            return attend(group_item[0], group_item[1], root_keyval)
        bottleneck = lax.map(jax.checkpoint(one_group), (queries, group_keyval)).reshape(-1, C_COARSE)
        return coarse.reshape(-1, C_COARSE) + matmul_high(bottleneck, weight_set[9])
    weight_set = (gain_leaf, w_qkv_leaf, w_out_leaf, w_pool1, w_pool2, w_pool3, gain_coarse, w_query, w_keyval, w_out)
    output, pullback = jax.vjp(forward, weight_set)
    gradient_set = pullback(cotangent)[0]
    return (output, gradient_set[0], gradient_set[1], gradient_set[2], gradient_set[3], gradient_set[4], gradient_set[5], gradient_set[6], gradient_set[7], gradient_set[8], gradient_set[9])
```

```python
import jax
import jax.numpy as jnp
from jax import lax
from jax.sharding import Mesh
from jax.sharding import PartitionSpec as P

HEAD = 32
BALL = 128
ROOT_DEV = 2
GRP = ("zh", "co")
LEAF = ("zl", "y", "x")
ALL = GRP + LEAF
N_LEAF = 32
N_GRP = 4
HEADS = 16

PREC = lax.Precision.HIGHEST


def mm(left, right):
    return jnp.dot(left, right, precision=PREC, preferred_element_type=jnp.float32)


def mm_t(left, right):
    return lax.dot_general(
        left, right, (((1,), (1,)), ((), ())), precision=PREC, preferred_element_type=jnp.float32
    )


def t_mm(left, right):
    return lax.dot_general(
        left, right, (((0,), (0,)), ((), ())), precision=PREC, preferred_element_type=jnp.float32
    )


def rms_scale(values, gain):
    return values * lax.rsqrt(jnp.mean(values * values, axis=-1, keepdims=True) + 1e-06) * gain


def leaf_front(ordered, gain_leaf, w_qkv_leaf, w_out_leaf, w_pool1, w_pool2, w_pool3):
    row_count, feature_width = ordered.shape
    head_count = feature_width // HEAD
    leaf_normed = rms_scale(ordered, gain_leaf)
    packed = mm(leaf_normed, w_qkv_leaf).reshape(row_count // BALL, BALL, 3, head_count, HEAD)
    queries = packed[:, :, 0] * HEAD ** (-0.5)
    scores = jnp.einsum("bihd,bjhd->bhij", queries, packed[:, :, 1], precision=PREC)
    weights = jax.nn.softmax(scores, axis=-1)
    attended = jnp.einsum("bhij,bjhd->bihd", weights, packed[:, :, 2], precision=PREC)
    leaf_mixed = ordered + mm(attended.reshape(row_count, feature_width), w_out_leaf)
    level_one = jax.nn.silu(mm(leaf_mixed.reshape(row_count // 4, -1), w_pool1))
    level_two = jax.nn.silu(mm(level_one.reshape(row_count // 16, -1), w_pool2))
    return mm(level_two.reshape(row_count // 64, -1), w_pool3)


def part(queries, keys, values, d_out):
    scores = mm_t(queries, keys) * HEAD ** (-0.5)
    weights = jax.nn.softmax(scores, axis=-1)
    out = mm(weights, values)
    d_values = t_mm(weights, d_out)
    d_weights = mm_t(d_out, values)
    d_scores = weights * (d_weights - jnp.sum(weights * d_weights, axis=-1, keepdims=True))
    d_scores = d_scores * HEAD ** (-0.5)
    return out, mm(d_scores, keys), t_mm(d_scores, queries), d_values


def heads_out(rows):
    return rows.reshape(rows.shape[0], HEADS, HEAD).transpose(1, 0, 2)


def heads_in(blocks):
    return blocks.transpose(1, 0, 2).reshape(blocks.shape[1], HEADS * HEAD)


def shards(
    features,
    tree_order,
    gain_leaf,
    w_qkv_leaf,
    w_out_leaf,
    w_pool1,
    w_pool2,
    w_pool3,
    gain_coarse,
    w_query,
    w_keyval,
    w_out,
    cotangent,
):
    half = lax.axis_index("x") % 2
    ordered = features[tree_order[0]]

    def front(front_weights):
        coarse = leaf_front(ordered, *front_weights[:6])
        coarse_normed = rms_scale(coarse, front_weights[6])
        block_means = jnp.mean(coarse.reshape(ROOT_DEV, -1, coarse.shape[-1]), axis=1)
        rows = jnp.concatenate([coarse_normed, rms_scale(block_means, front_weights[6])], axis=0)
        return coarse, rows

    front_weights = (gain_leaf, w_qkv_leaf, w_out_leaf, w_pool1, w_pool2, w_pool3, gain_coarse)
    (coarse, rows), pull_front = jax.vjp(front, front_weights)
    d_bottleneck = mm_t(cotangent, w_out)
    keyval = mm(rows, w_keyval)
    queries = mm(rows[:16], w_query)
    roots = lax.all_gather(keyval[16:].reshape(16, 128), GRP, axis=0, tiled=True).reshape(8, 1024)
    main = jnp.concatenate(
        [
            heads_out(queries),
            heads_out(keyval[:16, :512]),
            heads_out(keyval[:16, 512:]),
            heads_out(d_bottleneck),
        ],
        axis=-1,
    )
    side = jnp.concatenate([heads_out(roots[:, :512]), heads_out(roots[:, 512:])], axis=-1)
    side = jnp.concatenate([side, jnp.zeros_like(side)], axis=-1)
    message = jnp.concatenate([main, side], axis=1)
    message = jnp.broadcast_to(message[:, None], (HEADS, 2, 24, 128)).reshape(N_LEAF, 24, 128)
    got = lax.all_to_all(message, LEAF, 0, 0, tiled=True)
    mine = lax.dynamic_slice(got, (0, half * 8, 0), (N_LEAF, 8, 128)).reshape(256, 128)
    every = got[:, :16].reshape(512, 128)
    away = got[:, 16:].reshape(256, 128)
    q, d_o = mine[:, :32], mine[:, 96:]
    out_a, dq_a, dk_a, dv_a = part(q, every[:, 32:64], every[:, 64:96], d_o)
    out_b, dq_b, dk_b, dv_b = part(q, away[:, :32], away[:, 32:64], d_o)
    front_half = jnp.concatenate([out_a + out_b, dq_a + dq_b], axis=-1).reshape(N_LEAF, 8, 64)
    front_half = lax.dynamic_update_slice(
        jnp.zeros((N_LEAF, 16, 64), jnp.float32), front_half, (0, half * 8, 0)
    )
    back_half = jnp.concatenate([dk_a, dv_a], axis=-1).reshape(N_LEAF, 16, 64)
    side = jnp.concatenate([dk_b, dv_b], axis=-1).reshape(N_LEAF, 8, 64)
    side = jnp.concatenate([side, jnp.zeros_like(side)], axis=-1)
    message = jnp.concatenate([jnp.concatenate([front_half, back_half], axis=-1), side], axis=1)
    got = lax.all_to_all(message, LEAF, 0, 0, tiled=True)
    got = got.reshape(HEADS, 2, 24, 128)
    got = got[:, 0] + got[:, 1]
    bottleneck = heads_in(got[:, :16, :32])
    d_queries = heads_in(got[:, :16, 32:64])
    d_keyval = jnp.concatenate([heads_in(got[:, :16, 64:96]), heads_in(got[:, :16, 96:])], axis=-1)
    d_roots = jnp.concatenate([heads_in(got[:, 16:, :32]), heads_in(got[:, 16:, 32:64])], axis=-1)
    d_roots = lax.all_to_all(d_roots.reshape(64, 128), GRP, 0, 0, tiled=True)
    d_roots = jnp.sum(d_roots.reshape(N_GRP, 2, 1024), axis=0)
    d_keyval = jnp.concatenate([d_keyval, d_roots], axis=0)
    output = coarse + mm(bottleneck, w_out)
    grad_out = t_mm(bottleneck, cotangent)
    grad_query = t_mm(rows[:16], d_queries)
    grad_keyval = t_mm(rows, d_keyval)
    d_rows = mm_t(d_keyval, w_keyval)
    d_rows = d_rows + jnp.pad(mm_t(d_queries, w_query), ((0, 2), (0, 0)))
    grads = pull_front((cotangent, d_rows))[0]
    gains = jnp.concatenate([grads[0], grads[6], jnp.zeros((384,), jnp.float32)]).reshape(8, 128)
    low = jnp.concatenate([grads[2], gains], axis=0)
    totals = lax.psum(
        (grads[1], low, grads[3], grads[4], grads[5], grad_query, grad_keyval, grad_out), ALL
    )
    gains = totals[1][128:].reshape(1024)
    return (
        output,
        gains[:128],
        totals[0],
        totals[1][:128],
        totals[2],
        totals[3],
        totals[4],
        gains[128:640],
        totals[5],
        totals[6],
        totals[7],
    )


def solution(mesh):
    fine = Mesh(mesh.devices.reshape(2, 2, 2, 4, 4), ALL)
    cut = P(ALL, None)
    return jax.shard_map(
        shards,
        mesh=fine,
        in_specs=(cut, cut) + (P(),) * 10 + (cut,),
        out_specs=(cut,) + (P(),) * 10,
        check_vma=False,
    )
```

```python
import jax
import jax.numpy as jnp
from jax import lax
from jax.experimental import pallas as pl
from jax.experimental.pallas import tpu as pltpu
from jax.sharding import Mesh
from jax.sharding import PartitionSpec as P

GRP = ("zh", "co")
LEAF = ("zl", "y", "x")
ALL = GRP + LEAF
N_LEAF = 32
HEADS = 16
SCALE = 32 ** (-0.5)
F32 = jnp.float32


def split(value):
    high = value.astype(jnp.bfloat16)
    return high, (value - high.astype(F32)).astype(jnp.bfloat16)


def dot3(left, right, dims):
    left_high, left_low = split(left)
    right_high, right_low = split(right)
    go = lambda a, b: lax.dot_general(a, b, (dims, ((), ())), preferred_element_type=F32)
    return go(left_high, right_high) + (go(left_high, right_low) + go(left_low, right_high))


def mm(left, right):
    return dot3(left, right, ((1,), (0,)))


def mm_t(left, right):
    return dot3(left, right, ((1,), (1,)))


def t_mm(left, right):
    return dot3(left, right, ((0,), (0,)))


def full(left, right, dims):
    return lax.dot_general(
        left, right, (dims, ((), ())), precision=lax.Precision.HIGHEST, preferred_element_type=F32
    )


def mm6(left, right):
    return full(left, right, ((1,), (0,)))


def mm6_t(left, right):
    return full(left, right, ((1,), (1,)))


def t_mm6(left, right):
    return full(left, right, ((0,), (0,)))


def lanes(at):
    lane = lax.broadcasted_iota(jnp.int32, (1, 128), 1)
    return ((lane >= 32 * at) & (lane < 32 * at + 32)).astype(F32)


def turn(value, by):
    by = by % 128
    return value if by == 0 else pltpu.roll(value, by, 1)


def inverse_rms(values):
    return lax.rsqrt(jnp.mean(values * values, axis=-1, keepdims=True) + 1e-06)


def sigmoid(pre):
    return 1.0 / (1.0 + jnp.exp(-pre))


def softmax(scores):
    weights = jnp.exp(scores - jnp.max(scores, axis=-1, keepdims=True))
    return weights / jnp.sum(weights, axis=-1, keepdims=True)


def four(value):
    return jnp.concatenate([value * lanes(h) for h in range(4)], axis=0)


def slot_one(rows, at):
    return rows.reshape(8, 4, 32, rows.shape[-1])[:, at].reshape(256, rows.shape[-1])


def slot_two(rows, at):
    return rows.reshape(8, 4, 8, rows.shape[-1])[:, at].reshape(64, rows.shape[-1])


def stride_get(ref, at, stride):
    blocks = [ref[j, pl.ds(at, 8, stride=stride), :] for j in range(ref.shape[0])]
    return jnp.concatenate(blocks, axis=1)


def stride_put(ref, at, stride, value):
    for j in range(ref.shape[0]):
        ref[j, pl.ds(at, 8, stride=stride), :] = value[:, 128 * j : 128 * j + 128]


def put_blocks(ref, value):
    for j in range(ref.shape[0]):
        ref[j] = value[:, 128 * j : 128 * j + 128]


def get_blocks(ref):
    return jnp.concatenate([ref[j] for j in range(ref.shape[0])], axis=1)


def slot_three(ref, at):
    return jnp.concatenate([stride_get(ref, 2 * at + a, 8) for a in range(2)], axis=0)


def forward_kernel(
    order, features, gain_leaf, w_qkv, w_out_leaf, w_one, w_two, w_three, gain_coarse, w_query,
    w_keyval, w_out, cotangent,
    unit, packed, weights, attended, mixed, pre_one, pre_two, two, coarse, rows, message, roots,
    ordered, natural,
):
    def fetch(step, carry):
        ball, rest = step // 16, step % 16
        base = ball * 128 + (rest % 4) * 4 + rest // 4
        for d2 in range(4):
            for a in range(2):
                source = order[0, base + 64 * a + 16 * d2]
                ordered[pl.ds(step * 8 + 2 * d2 + a, 1), :] = features[pl.ds(source, 1), :]
        return carry

    lax.fori_loop(0, 128, fetch, 0)
    unit[...] = ordered[...] * inverse_rms(ordered[...])
    packed[...] = mm6(unit[...] * gain_leaf[...], w_qkv[...])

    def ball(step, carry):
        at = pl.ds(step * 128, 128)
        values = packed[at, 256:]
        scores = mm6_t(four(packed[at, :128] * SCALE), packed[at, 128:256])
        probs = softmax(scores)
        weights[pl.ds(step * 512, 512), :] = probs
        wide = jnp.concatenate([probs[128 * h : 128 * h + 128] for h in range(4)], axis=1)
        attended[at, :] = mm6(wide, four(values))
        return carry

    lax.fori_loop(0, 8, ball, 0)
    joined = ordered[...] + mm6(attended[...], w_out_leaf[...])
    mixed[...] = joined
    pre = sum(mm6(slot_one(joined, d), w_one[128 * d : 128 * d + 128, :]) for d in range(4))
    pre_one[...] = pre
    one = pre * sigmoid(pre)
    pre = sum(mm6(slot_two(one, d), w_two[256 * d : 256 * d + 256, :]) for d in range(4))
    pre_two[...] = pre
    put_blocks(two, pre * sigmoid(pre))
    top = sum(mm6(slot_three(two, d), w_three[384 * d : 384 * d + 384, :]) for d in range(4))
    for a in range(2):
        stride_put(natural, a, 2, top[8 * a : 8 * a + 8])
    top = get_blocks(natural)
    coarse[...] = top
    means = jnp.concatenate(
        [jnp.mean(top[8 * r : 8 * r + 8], axis=0, keepdims=True) for r in range(2)]
        + [jnp.zeros((6, 512), F32)],
        axis=0,
    )
    normed = jnp.concatenate([top * inverse_rms(top), means * inverse_rms(means)], axis=0)
    normed = normed * gain_coarse[...]
    rows[...] = normed
    queries = mm6(normed[:16], w_query[...])
    keyval = mm6(normed, w_keyval[...])
    d_bottleneck = mm6_t(cotangent[...], w_out[...])
    parts = (queries, keyval[:16, :512], keyval[:16, 512:], d_bottleneck)
    for h in range(HEADS):
        block = slice(128 * (h // 4), 128 * (h // 4) + 128)
        message[h] = sum(
            turn(part[:, block], 32 * (c - h % 4)) * lanes(c) for c, part in enumerate(parts)
        )
    for j in range(8):
        roots[2 * j : 2 * j + 2, :] = keyval[16:18, 128 * j : 128 * j + 128]
    for j in range(4):
        roots[16 + 2 * j : 18 + 2 * j, :] = normed[16:18, 128 * j : 128 * j + 128]


def message_kernel(main, roots, message, root_rows):
    block = lambda j: roots[:, 2 * j : 2 * j + 2, :].reshape(8, 128)
    for h in range(HEADS):
        side = turn(block(h // 4), -32 * (h % 4)) * lanes(0)
        side = side + turn(block(4 + h // 4), 32 - 32 * (h % 4)) * lanes(1)
        for half in range(2):
            message[2 * h + half, :16, :] = main[h]
            message[2 * h + half, 16:, :] = side
    for j in range(4):
        root_rows[:, 128 * j : 128 * j + 128] = block(8 + j)


def attend_kernel(half, got, message):
    at = pl.multiple_of(half[0] * 8, 8)
    mine = got[:, pl.ds(at, 8), :].reshape(256, 128)
    every = got[:, :16, :].reshape(512, 128)
    away = got[:, 16:, :].reshape(256, 128)
    queries = mine * lanes(0) * SCALE
    d_out = mine * lanes(3)

    def scores_of(keys, values):
        probs = softmax(mm6_t(queries, keys))
        d_probs = mm6_t(d_out, values)
        d_scores = probs * (d_probs - jnp.sum(probs * d_probs, axis=-1, keepdims=True))
        return probs, d_scores * SCALE

    probs, d_scores = scores_of(turn(every, -32), turn(every, 32))
    front = mm6(probs, turn(every, -64) * lanes(0)) + mm6(d_scores, every * lanes(1))
    back = t_mm6(d_scores, turn(mine, 64) * lanes(2)) + t_mm6(probs, d_out)
    probs, d_scores = scores_of(away, turn(away, 64))
    front = front + mm6(probs, turn(away, -32) * lanes(0))
    front = front + mm6(d_scores, turn(away, 32) * lanes(1))
    side = t_mm6(d_scores, mine * lanes(0)) + t_mm6(probs, turn(mine, 64) * lanes(1))
    message[:, :16, :] = back.reshape(N_LEAF, 16, 128)
    message[:, pl.ds(at, 8), :] = message[:, pl.ds(at, 8), :] + front.reshape(N_LEAF, 8, 128)
    message[:, 16:, :] = side.reshape(N_LEAF, 8, 128)


def unpack_kernel(got, bottleneck, d_queries, d_keyval, d_roots):
    for block in range(4):
        heads = [got[2 * h] + got[2 * h + 1] for h in range(4 * block, 4 * block + 4)]
        pick = lambda c, rows: sum(
            turn(heads[k][rows], 32 * (k - c)) * lanes(k) for k in range(4)
        )
        own, far = slice(0, 16), slice(16, 24)
        at = slice(128 * block, 128 * block + 128)
        bottleneck[:, at] = pick(0, own)
        d_queries[:, at] = pick(1, own)
        d_keyval[:, at] = pick(2, own)
        d_keyval[:, 512 + 128 * block : 640 + 128 * block] = pick(3, own)
        d_roots[:, 2 * block : 2 * block + 2, :] = pick(0, far).reshape(4, 2, 128)
        d_roots[:, 8 + 2 * block : 10 + 2 * block, :] = pick(1, far).reshape(4, 2, 128)


def upper_kernel(coarse, bottleneck, d_queries, rows, cotangent, w_out, output, grad_out, grad_query):
    output[...] = coarse[...] + mm(bottleneck[...], w_out[...])
    grad_out[...] = t_mm(bottleneck[...], cotangent[...])
    grad_query[...] = t_mm(rows[:16, :], d_queries[...])


def rms_backward(d_normed, values, gain):
    scale = inverse_rms(values)
    unit = values * scale
    d_unit = d_normed * gain
    d_values = scale * (d_unit - unit * jnp.mean(d_unit * unit, axis=-1, keepdims=True))
    return d_values, jnp.sum(d_normed * unit, axis=0, keepdims=True)


def backward_kernel(
    d_roots, d_queries, d_keyval, rows, coarse, cotangent, gain_coarse, w_query, w_keyval,
    w_three, w_two, w_one, w_out_leaf, w_qkv, gain_leaf,
    unit, packed, weights, attended, mixed, pre_one, pre_two, two,
    grad_keyval, grad_three, grad_two, grad_one, grad_out_leaf, grad_qkv, gains,
    d_coarse, d_two, d_packed, d_attended,
):
    far = jnp.sum(d_roots[...], axis=0)
    far = jnp.concatenate([far[2 * j : 2 * j + 2] for j in range(8)], axis=1)
    d_kv = jnp.concatenate([d_keyval[...], far, jnp.zeros((6, 1024), F32)], axis=0)
    grad_keyval[...] = t_mm(rows[...], d_kv)
    d_rows = mm_t(d_kv, w_keyval[...])
    top = coarse[...]
    d_top, gain_a = rms_backward(
        d_rows[:16] + mm_t(d_queries[...], w_query[...]), top, gain_coarse[...]
    )
    means = jnp.concatenate(
        [jnp.mean(top[8 * r : 8 * r + 8], axis=0, keepdims=True) for r in range(2)], axis=0
    )
    d_means, gain_b = rms_backward(d_rows[16:18], means, gain_coarse[...])
    d_means = d_means * 0.125
    d_means = jnp.concatenate(
        [jnp.broadcast_to(d_means[r : r + 1], (8, 512)) for r in range(2)], axis=0
    )
    put_blocks(d_coarse, cotangent[...] + d_top + d_means)
    gain_c = gain_a + gain_b

    d_top = jnp.concatenate([stride_get(d_coarse, a, 2) for a in range(2)], axis=0)
    for d in range(4):
        at = slice(384 * d, 384 * d + 384)
        grad_three[at, :] = t_mm(slot_three(two, d), d_top)
        part = mm_t(d_top, w_three[at, :])
        for a in range(2):
            stride_put(d_two, 2 * d + a, 8, part[8 * a : 8 * a + 8])
    pre = pre_two[...]
    gate = sigmoid(pre)
    d_pre = get_blocks(d_two) * (gate * (1.0 + pre * (1.0 - gate)))
    pre = pre_one[...]
    gate = sigmoid(pre)
    one = pre * gate
    parts = []
    for d in range(4):
        at = slice(256 * d, 256 * d + 256)
        grad_two[at, :] = t_mm(slot_two(one, d), d_pre)
        parts.append(mm_t(d_pre, w_two[at, :]).reshape(8, 1, 8, 256))
    d_one = jnp.concatenate(parts, axis=1).reshape(256, 256)
    d_pre = d_one * (gate * (1.0 + pre * (1.0 - gate)))
    joined = mixed[...]
    parts = []
    for d in range(4):
        at = slice(128 * d, 128 * d + 128)
        grad_one[at, :] = t_mm(slot_one(joined, d), d_pre)
        parts.append(mm_t(d_pre, w_one[at, :]).reshape(8, 1, 32, 128))
    d_mixed = jnp.concatenate(parts, axis=1).reshape(1024, 128)
    grad_out_leaf[...] = t_mm(attended[...], d_mixed)
    d_attended[...] = mm_t(d_mixed, w_out_leaf[...])

    def ball(step, carry):
        at = pl.ds(step * 128, 128)
        probs = weights[pl.ds(step * 512, 512), :]
        d_out = four(d_attended[at, :])
        d_probs = mm6_t(d_out, packed[at, 256:])
        d_scores = probs * (d_probs - jnp.sum(probs * d_probs, axis=-1, keepdims=True)) * SCALE
        wide = jnp.concatenate([d_scores[128 * h : 128 * h + 128] for h in range(4)], axis=1)
        d_packed[at, :128] = mm(wide, four(packed[at, 128:256]))
        d_packed[at, 128:256] = t_mm(d_scores, four(packed[at, :128]))
        d_packed[at, 256:] = t_mm(probs, d_out)
        return carry

    lax.fori_loop(0, 8, ball, 0)
    grad_qkv[...] = t_mm(unit[...] * gain_leaf[...], d_packed[...])
    d_normed = mm_t(d_packed[...], w_qkv[...])
    gains[...] = jnp.concatenate(
        [jnp.sum(d_normed * unit[...], axis=0, keepdims=True)]
        + [gain_c[:, 128 * j : 128 * j + 128] for j in range(4)]
        + [jnp.zeros((3, 128), F32)],
        axis=0,
    )


def call(kernel, outs, scratch=(), smem_first=False):
    shapes = [jax.ShapeDtypeStruct(shape, F32) for shape in outs]

    def run(*args):
        specs = [pl.BlockSpec(memory_space=pltpu.VMEM)] * len(args)
        if smem_first:
            specs[0] = pl.BlockSpec(memory_space=pltpu.SMEM)
        return pl.pallas_call(
            kernel,
            out_shape=shapes,
            in_specs=specs,
            out_specs=[pl.BlockSpec(memory_space=pltpu.VMEM)] * len(shapes),
            scratch_shapes=[pltpu.VMEM(shape, F32) for shape in scratch],
            compiler_params=pltpu.CompilerParams(vmem_limit_bytes=56 * 2**20),
        )(*args)

    return run


def shards(
    features, tree_order, gain_leaf, w_qkv, w_out_leaf, w_one, w_two, w_three, gain_coarse,
    w_query, w_keyval, w_out, cotangent,
):
    half = (lax.axis_index("x") % 2).astype(jnp.int32).reshape(1)
    gain_leaf = gain_leaf.reshape(1, 128)
    gain_coarse = gain_coarse.reshape(1, 512)
    saved_shapes = [
        (1024, 128), (1024, 384), (4096, 128), (1024, 128), (1024, 128), (256, 256), (64, 384),
        (3, 64, 128),
    ]
    *saved, coarse, rows, main, roots = call(
        forward_kernel,
        saved_shapes + [(16, 512), (24, 512), (HEADS, 16, 128), (24, 128)],
        [(1024, 128), (4, 16, 128)],
        True,
    )(
        tree_order, features, gain_leaf, w_qkv, w_out_leaf, w_one, w_two, w_three, gain_coarse,
        w_query, w_keyval, w_out, cotangent,
    )
    roots = lax.all_gather(roots, GRP, axis=0)
    message, root_rows = call(message_kernel, [(N_LEAF, 24, 128), (8, 512)])(main, roots)
    got = lax.all_to_all(message, LEAF, 0, 0, tiled=True)
    message = call(attend_kernel, [(N_LEAF, 24, 128)], (), True)(half, got)[0]
    got = lax.all_to_all(message, LEAF, 0, 0, tiled=True)
    bottleneck, d_queries, d_keyval, d_roots = call(
        unpack_kernel, [(16, 512), (16, 512), (16, 1024), (4, 16, 128)]
    )(got)
    d_roots = lax.all_to_all(d_roots, GRP, 0, 0, tiled=True)
    output, grad_out, grad_query = call(upper_kernel, [(16, 512), (512, 512), (512, 512)])(
        coarse, bottleneck, d_queries, rows, cotangent, w_out
    )
    grads = call(
        backward_kernel,
        [(512, 1024), (1536, 512), (1024, 384), (512, 256), (128, 128), (128, 384), (8, 128)],
        [(4, 16, 128), (3, 64, 128), (1024, 384), (1024, 128)],
    )(
        d_roots, d_queries, d_keyval, rows, coarse, cotangent, gain_coarse, w_query, w_keyval,
        w_three, w_two, w_one, w_out_leaf, w_qkv, gain_leaf, *saved,
    )
    grad_keyval, grad_three, grad_two, grad_one, grad_out_leaf, grad_qkv, gains = grads
    low = jnp.concatenate([grad_out_leaf, gains], axis=0)
    totals = lax.psum(
        (grad_qkv, low, grad_one, grad_two, grad_three, grad_query, grad_keyval, grad_out), ALL
    )
    low = totals[1]
    return (
        output,
        low[128],
        totals[0],
        low[:128],
        totals[2],
        totals[3],
        totals[4],
        low[129:133].reshape(512),
        totals[5],
        totals[6],
        totals[7],
    )


def solution(mesh):
    fine = Mesh(mesh.devices.reshape(2, 2, 2, 4, 4), ALL)
    cut = P(ALL, None)
    return jax.shard_map(
        shards,
        mesh=fine,
        in_specs=(cut, cut) + (P(),) * 10 + (cut,),
        out_specs=(cut,) + (P(),) * 10,
        check_vma=False,
    )
```

```python
import jax
import jax.numpy as jnp
from jax import lax
from jax.experimental import pallas as pl
from jax.experimental.pallas import tpu as pltpu
from jax.sharding import Mesh
from jax.sharding import PartitionSpec as P

GRP = ("zh", "co")
LEAF = ("zl", "y", "x")
ALL = GRP + LEAF
CHIPS = ("zh",) + LEAF
N_LEAF = 32
HEADS = 16
SCALE = 32 ** (-0.5)
F32 = jnp.float32


def split(value):
    high = value.astype(jnp.bfloat16)
    return high, (value - high.astype(F32)).astype(jnp.bfloat16)


def dot3(left, right, dims):
    left_high, left_low = split(left)
    right_high, right_low = split(right)
    go = lambda a, b: lax.dot_general(a, b, (dims, ((), ())), preferred_element_type=F32)
    return go(left_high, right_high) + (go(left_high, right_low) + go(left_low, right_high))


def mm(left, right):
    return dot3(left, right, ((1,), (0,)))


def mm_t(left, right):
    return dot3(left, right, ((1,), (1,)))


def t_mm(left, right):
    return dot3(left, right, ((0,), (0,)))


def full(left, right, dims):
    return lax.dot_general(
        left, right, (dims, ((), ())), precision=lax.Precision.HIGHEST, preferred_element_type=F32
    )


def mm6(left, right):
    return full(left, right, ((1,), (0,)))


def mm6_t(left, right):
    return full(left, right, ((1,), (1,)))


def t_mm6(left, right):
    return full(left, right, ((0,), (0,)))


def lanes(at):
    lane = lax.broadcasted_iota(jnp.int32, (1, 128), 1)
    return ((lane >= 32 * at) & (lane < 32 * at + 32)).astype(F32)


def turn(value, by):
    by = by % 128
    return value if by == 0 else pltpu.roll(value, by, 1)


def inverse_rms(values):
    return lax.rsqrt(jnp.mean(values * values, axis=-1, keepdims=True) + 1e-06)


def sigmoid(pre):
    return 1.0 / (1.0 + jnp.exp(-pre))


def softmax(scores):
    weights = jnp.exp(scores - jnp.max(scores, axis=-1, keepdims=True))
    return weights / jnp.sum(weights, axis=-1, keepdims=True)


def four(value):
    return jnp.concatenate([value * lanes(h) for h in range(4)], axis=0)


def slot_one(rows, at):
    return rows.reshape(8, 4, 32, rows.shape[-1])[:, at].reshape(256, rows.shape[-1])


def slot_two(rows, at):
    return rows.reshape(8, 4, 8, rows.shape[-1])[:, at].reshape(64, rows.shape[-1])


def stride_get(ref, at, stride):
    blocks = [ref[j, pl.ds(at, 8, stride=stride), :] for j in range(ref.shape[0])]
    return jnp.concatenate(blocks, axis=1)


def stride_put(ref, at, stride, value):
    for j in range(ref.shape[0]):
        ref[j, pl.ds(at, 8, stride=stride), :] = value[:, 128 * j : 128 * j + 128]


def put_blocks(ref, value):
    for j in range(ref.shape[0]):
        ref[j] = value[:, 128 * j : 128 * j + 128]


def get_blocks(ref):
    return jnp.concatenate([ref[j] for j in range(ref.shape[0])], axis=1)


def slot_three(ref, at):
    return jnp.concatenate([stride_get(ref, 2 * at + a, 8) for a in range(2)], axis=0)


def forward_kernel(
    order, features, gain_leaf, w_qkv, w_out_leaf, w_one, w_two, w_three, gain_coarse, w_query,
    w_keyval, w_out, cotangent,
    unit, packed, weights, attended, mixed, pre_one, pre_two, two, coarse, rows, message, roots,
    ordered, natural,
):
    def fetch(step, carry):
        ball, rest = step // 16, step % 16
        base = ball * 128 + (rest % 4) * 4 + rest // 4
        for d2 in range(4):
            for a in range(2):
                source = order[0, base + 64 * a + 16 * d2]
                ordered[pl.ds(step * 8 + 2 * d2 + a, 1), :] = features[pl.ds(source, 1), :]
        return carry

    lax.fori_loop(0, 128, fetch, 0)
    unit[...] = ordered[...] * inverse_rms(ordered[...])
    packed[...] = mm6(unit[...] * gain_leaf[...], w_qkv[...])

    def ball(step, carry):
        at = pl.ds(step * 128, 128)
        values = packed[at, 256:]
        scores = mm6_t(four(packed[at, :128] * SCALE), packed[at, 128:256])
        probs = softmax(scores)
        weights[pl.ds(step * 512, 512), :] = probs
        wide = jnp.concatenate([probs[128 * h : 128 * h + 128] for h in range(4)], axis=1)
        attended[at, :] = mm6(wide, four(values))
        return carry

    lax.fori_loop(0, 8, ball, 0)
    joined = ordered[...] + mm6(attended[...], w_out_leaf[...])
    mixed[...] = joined
    pre = sum(mm6(slot_one(joined, d), w_one[128 * d : 128 * d + 128, :]) for d in range(4))
    pre_one[...] = pre
    one = pre * sigmoid(pre)
    pre = sum(mm6(slot_two(one, d), w_two[256 * d : 256 * d + 256, :]) for d in range(4))
    pre_two[...] = pre
    put_blocks(two, pre * sigmoid(pre))
    top = sum(mm6(slot_three(two, d), w_three[384 * d : 384 * d + 384, :]) for d in range(4))
    for a in range(2):
        stride_put(natural, a, 2, top[8 * a : 8 * a + 8])
    top = get_blocks(natural)
    coarse[...] = top
    means = jnp.concatenate(
        [jnp.mean(top[8 * r : 8 * r + 8], axis=0, keepdims=True) for r in range(2)]
        + [jnp.zeros((6, 512), F32)],
        axis=0,
    )
    normed = jnp.concatenate([top * inverse_rms(top), means * inverse_rms(means)], axis=0)
    normed = normed * gain_coarse[...]
    rows[...] = normed
    queries = mm6(normed[:16], w_query[...])
    keyval = mm6(normed, w_keyval[...])
    d_bottleneck = mm6_t(cotangent[...], w_out[...])
    parts = (queries, keyval[:16, :512], keyval[:16, 512:], d_bottleneck)
    for h in range(HEADS):
        block = slice(128 * (h // 4), 128 * (h // 4) + 128)
        message[h] = sum(
            turn(part[:, block], 32 * (c - h % 4)) * lanes(c) for c, part in enumerate(parts)
        )
    for j in range(8):
        roots[2 * j : 2 * j + 2, :] = keyval[16:18, 128 * j : 128 * j + 128]
    for j in range(4):
        roots[16 + 2 * j : 18 + 2 * j, :] = normed[16:18, 128 * j : 128 * j + 128]


def message_kernel(group, main, roots, one, two, three, message, root_rows, sorted_roots):
    for k, part in enumerate((roots, one, two, three)):
        sorted_roots[group[0] ^ k] = part[...]
    roots = sorted_roots
    block = lambda j: roots[:, 2 * j : 2 * j + 2, :].reshape(8, 128)
    for h in range(HEADS):
        side = turn(block(h // 4), -32 * (h % 4)) * lanes(0)
        side = side + turn(block(4 + h // 4), 32 - 32 * (h % 4)) * lanes(1)
        for half in range(2):
            message[2 * h + half, :16, :] = main[h]
            message[2 * h + half, 16:, :] = side
    for j in range(4):
        root_rows[:, 128 * j : 128 * j + 128] = block(8 + j)


def attend_kernel(half, got, message):
    at = pl.multiple_of(half[0] * 8, 8)
    mine = got[:, pl.ds(at, 8), :].reshape(256, 128)
    every = got[:, :16, :].reshape(512, 128)
    away = got[:, 16:, :].reshape(256, 128)
    queries = mine * lanes(0) * SCALE
    d_out = mine * lanes(3)

    def scores_of(keys, values):
        probs = softmax(mm6_t(queries, keys))
        d_probs = mm6_t(d_out, values)
        d_scores = probs * (d_probs - jnp.sum(probs * d_probs, axis=-1, keepdims=True))
        return probs, d_scores * SCALE

    probs, d_scores = scores_of(turn(every, -32), turn(every, 32))
    front = mm6(probs, turn(every, -64) * lanes(0)) + mm6(d_scores, every * lanes(1))
    back = t_mm6(d_scores, turn(mine, 64) * lanes(2)) + t_mm6(probs, d_out)
    probs, d_scores = scores_of(away, turn(away, 64))
    front = front + mm6(probs, turn(away, -32) * lanes(0))
    front = front + mm6(d_scores, turn(away, 32) * lanes(1))
    side = t_mm6(d_scores, mine * lanes(0)) + t_mm6(probs, turn(mine, 64) * lanes(1))
    message[:, :16, :] = back.reshape(N_LEAF, 16, 128)
    message[:, pl.ds(at, 8), :] = message[:, pl.ds(at, 8), :] + front.reshape(N_LEAF, 8, 128)
    message[:, 16:, :] = side.reshape(N_LEAF, 8, 128)


def unpack_kernel(got, rows, root_rows, cotangent, bottleneck, d_queries, d_keyval, d_roots, pack):
    pack[16:, :1024] = jnp.zeros((8, 1024), F32)
    pack[16:, 2560:] = jnp.zeros((8, 512), F32)
    pack[:16, 2048:2560] = rows[:16, :]
    pack[16:, 2048:2560] = root_rows[...]
    pack[:16, 2560:] = cotangent[...]
    for block in range(4):
        heads = [got[2 * h] + got[2 * h + 1] for h in range(4 * block, 4 * block + 4)]
        pick = lambda c, rows: sum(
            turn(heads[k][rows], 32 * (k - c)) * lanes(k) for k in range(4)
        )
        own, far = slice(0, 16), slice(16, 24)
        for c, ref in enumerate((bottleneck, d_queries, d_keyval, d_keyval)):
            at = 128 * block + (512 if c == 3 else 0)
            value = pick(c, own)
            ref[:, at : at + 128] = value
            pack[:16, 512 * c + 128 * block : 512 * c + 128 * block + 128] = value
        for c in range(2):
            value = pick(c, far)
            at = 8 * c + 2 * block
            d_roots[:, at : at + 2, :] = value.reshape(4, 2, 128)
            at = 1024 + 512 * c + 128 * block
            pack[16:, at : at + 128] = value


def upper_kernel(core, coarse, bottleneck, w_out, mine, other, output, grads):
    output[...] = coarse[...] + mm(bottleneck[...], w_out[...])
    both = lambda at, width: jnp.concatenate(
        [mine[:, pl.ds(at, width)], other[:, pl.ds(at, width)]], axis=0
    )
    half = lambda at, width: both(pl.multiple_of(at + core[0] * width, 128), width)
    normed = both(2048, 512)
    grads[:, :256] = t_mm(both(0, 512), half(2560, 256))
    grads[:, 256:512] = t_mm(normed, half(512, 256))
    grads[:, 512:] = t_mm(normed, half(1024, 512))


def assemble_upper_kernel(core, mine, other, grad_query, grad_keyval, grad_out):
    def fill(half, source):
        grad_out[:, 256 * half : 256 * half + 256] = source[:, :256]
        grad_query[:, 256 * half : 256 * half + 256] = source[:, 256:512]
        grad_keyval[:, 512 * half : 512 * half + 512] = source[:, 512:]

    for half in range(2):

        @pl.when(core[0] == half)
        def _():
            fill(half, mine)
            fill(1 - half, other)


def rms_backward(d_normed, values, gain):
    scale = inverse_rms(values)
    unit = values * scale
    d_unit = d_normed * gain
    d_values = scale * (d_unit - unit * jnp.mean(d_unit * unit, axis=-1, keepdims=True))
    return d_values, jnp.sum(d_normed * unit, axis=0, keepdims=True)


def backward_kernel(
    group, d_roots, roots_one, roots_two, roots_three, d_queries, d_keyval, rows, coarse, cotangent, gain_coarse, w_query, w_keyval,
    w_three, w_two, w_one, w_out_leaf, w_qkv, gain_leaf,
    unit, packed, weights, attended, mixed, pre_one, pre_two, two,
    keep, send,
    d_coarse, d_two, d_packed, d_attended,
):
    def put(half, chips, at, value):
        chips, at = pl.ds(*chips), pl.ds(*at)

        @pl.when(core == half)
        def _():
            keep[chips, at, :] = value

        @pl.when(core != half)
        def _():
            send[chips, at, :] = value

    core = group[0] % 2
    far = sum(ref[group[0]] for ref in (d_roots, roots_one, roots_two, roots_three))
    far = jnp.concatenate([far[2 * j : 2 * j + 2] for j in range(8)], axis=1)
    d_kv = jnp.concatenate([d_keyval[...], far, jnp.zeros((6, 1024), F32)], axis=0)
    d_rows = mm_t(d_kv, w_keyval[...])
    top = coarse[...]
    d_top, gain_a = rms_backward(
        d_rows[:16] + mm_t(d_queries[...], w_query[...]), top, gain_coarse[...]
    )
    means = jnp.concatenate(
        [jnp.mean(top[8 * r : 8 * r + 8], axis=0, keepdims=True) for r in range(2)], axis=0
    )
    d_means, gain_b = rms_backward(d_rows[16:18], means, gain_coarse[...])
    d_means = d_means * 0.125
    d_means = jnp.concatenate(
        [jnp.broadcast_to(d_means[r : r + 1], (8, 512)) for r in range(2)], axis=0
    )
    put_blocks(d_coarse, cotangent[...] + d_top + d_means)
    gain_c = gain_a + gain_b

    d_top = jnp.concatenate([stride_get(d_coarse, a, 2) for a in range(2)], axis=0)
    for d in range(4):
        at = slice(384 * d, 384 * d + 384)
        grad = t_mm(slot_three(two, d), d_top)
        for i in range(4):
            block = grad[:, 128 * i : 128 * i + 128].reshape(16, 24, 128)
            put(i // 2, (16 * d, 16), (24 * (i % 2), 24), block)
        part = mm_t(d_top, w_three[at, :])
        for a in range(2):
            stride_put(d_two, 2 * d + a, 8, part[8 * a : 8 * a + 8])
    pre = pre_two[...]
    gate = sigmoid(pre)
    d_pre = get_blocks(d_two) * (gate * (1.0 + pre * (1.0 - gate)))
    pre = pre_one[...]
    gate = sigmoid(pre)
    one = pre * gate
    parts = []
    for d in range(4):
        at = slice(256 * d, 256 * d + 256)
        grad = t_mm(slot_two(one, d), d_pre)
        for i in range(3):
            block = grad[:, 128 * i : 128 * i + 128].reshape(32, 8, 128)
            put(d // 2, (32 * (d % 2), 32), (48 + 8 * i, 8), block)
        parts.append(mm_t(d_pre, w_two[at, :]).reshape(8, 1, 8, 256))
    d_one = jnp.concatenate(parts, axis=1).reshape(256, 256)
    d_pre = d_one * (gate * (1.0 + pre * (1.0 - gate)))
    joined = mixed[...]
    parts = []
    for d in range(4):
        at = slice(128 * d, 128 * d + 128)
        grad = t_mm(slot_one(joined, d), d_pre)
        for i in range(2):
            put(i, (16 * d, 16), (72, 8), grad[:, 128 * i : 128 * i + 128].reshape(16, 8, 128))
        parts.append(mm_t(d_pre, w_one[at, :]).reshape(8, 1, 32, 128))
    d_mixed = jnp.concatenate(parts, axis=1).reshape(1024, 128)
    grad_out_leaf = t_mm(attended[...], d_mixed)
    d_attended[...] = mm_t(d_mixed, w_out_leaf[...])

    def ball(step, carry):
        at = pl.ds(step * 128, 128)
        probs = weights[pl.ds(step * 512, 512), :]
        d_out = four(d_attended[at, :])
        d_probs = mm6_t(d_out, packed[at, 256:])
        d_scores = probs * (d_probs - jnp.sum(probs * d_probs, axis=-1, keepdims=True)) * SCALE
        wide = jnp.concatenate([d_scores[128 * h : 128 * h + 128] for h in range(4)], axis=1)
        d_packed[at, :128] = mm(wide, four(packed[at, 128:256]))
        d_packed[at, 128:256] = t_mm(d_scores, four(packed[at, :128]))
        d_packed[at, 256:] = t_mm(probs, d_out)
        return carry

    lax.fori_loop(0, 8, ball, 0)
    grad_qkv = t_mm(unit[...] * gain_leaf[...], d_packed[...])
    blocks = [grad_qkv[:, 128 * i : 128 * i + 128] for i in range(3)] + [grad_out_leaf]
    for i, block in enumerate(blocks):
        put(i // 2, (16 * (i % 2), 16), (80, 8), block.reshape(16, 8, 128))
    d_normed = mm_t(d_packed[...], w_qkv[...])
    gains = jnp.concatenate(
        [jnp.sum(d_normed * unit[...], axis=0, keepdims=True)]
        + [gain_c[:, 128 * j : 128 * j + 128] for j in range(4)]
        + [jnp.zeros((3, 128), F32)],
        axis=0,
    )
    put(0, (32, 1), (80, 8), gains.reshape(1, 8, 128))
    put(0, (33, 31), (80, 8), jnp.zeros((31, 8, 128), F32))
    put(1, (32, 32), (80, 8), jnp.zeros((32, 8, 128), F32))


def assemble_kernel(
    core, mine, other,
    gain_leaf, gain_coarse, grad_qkv, grad_out_leaf, grad_one, grad_two, grad_three,
):
    def fill(half, source):
        for i in range(2):
            at = 256 * half + 128 * i
            grad_three[:, at : at + 128] = source[:, 24 * i : 24 * i + 24, :].reshape(1536, 128)
        for i in range(3):
            block = source[:, 48 + 8 * i : 56 + 8 * i, :].reshape(512, 128)
            grad_two[512 * half : 512 * half + 512, 128 * i : 128 * i + 128] = block
        grad_one[:, 128 * half : 128 * half + 128] = source[:, 72:80, :].reshape(512, 128)
        first = source[0:16, 80:88, :].reshape(128, 128)
        second = source[16:32, 80:88, :].reshape(128, 128)
        if half == 0:
            grad_qkv[:, :128] = first
            grad_qkv[:, 128:256] = second
            gain_leaf[...] = source[32, 80, :]
            for i in range(4):
                gain_coarse[128 * i : 128 * i + 128] = source[32, 81 + i, :]
        else:
            grad_qkv[:, 256:] = first
            grad_out_leaf[...] = second

    for half in range(2):

        @pl.when(core[0] == half)
        def _():
            fill(half, mine)
            fill(1 - half, other)


def call(kernel, outs, scratch=(), smem_first=False, cost=None):
    shapes = [jax.ShapeDtypeStruct(shape, F32) for shape in outs]

    def run(*args):
        specs = [pl.BlockSpec(memory_space=pltpu.VMEM)] * len(args)
        if smem_first:
            specs[0] = pl.BlockSpec(memory_space=pltpu.SMEM)
        return pl.pallas_call(
            kernel,
            out_shape=shapes,
            in_specs=specs,
            out_specs=[pl.BlockSpec(memory_space=pltpu.VMEM)] * len(shapes),
            scratch_shapes=[pltpu.VMEM(shape, F32) for shape in scratch],
            cost_estimate=cost,
            compiler_params=pltpu.CompilerParams(vmem_limit_bytes=56 * 2**20),
        )(*args)

    return run


def group_swaps(value):
    return [lax.ppermute(value, GRP, [(i, i ^ k) for i in range(4)]) for k in range(1, 4)]


def spread(value, axes, parts):
    wide = jnp.broadcast_to(value[None], (parts,) + value.shape)
    return lax.all_to_all(wide, axes, 0, 0, tiled=True)


def shards(
    features, tree_order, gain_leaf, w_qkv, w_out_leaf, w_one, w_two, w_three, gain_coarse,
    w_query, w_keyval, w_out, cotangent,
):
    half = (lax.axis_index("x") % 2).astype(jnp.int32).reshape(1)
    group = lax.axis_index(GRP).astype(jnp.int32).reshape(1)
    core = lax.axis_index("co").astype(jnp.int32).reshape(1)
    gain_leaf = gain_leaf.reshape(1, 128)
    gain_coarse = gain_coarse.reshape(1, 512)
    saved_shapes = [
        (1024, 128), (1024, 384), (4096, 128), (1024, 128), (1024, 128), (256, 256), (64, 384),
        (3, 64, 128),
    ]
    *saved, coarse, rows, main, roots = call(
        forward_kernel,
        saved_shapes + [(16, 512), (24, 512), (HEADS, 16, 128), (24, 128)],
        [(1024, 128), (4, 16, 128)],
        True,
    )(
        tree_order, features, gain_leaf, w_qkv, w_out_leaf, w_one, w_two, w_three, gain_coarse,
        w_query, w_keyval, w_out, cotangent,
    )
    message, root_rows = call(
        message_kernel, [(N_LEAF, 24, 128), (8, 512)], [(4, 24, 128)], True
    )(group, main, roots, *group_swaps(roots))
    got = lax.all_to_all(message, LEAF, 0, 0, tiled=True)
    message = call(attend_kernel, [(N_LEAF, 24, 128)], (), True)(half, got)[0]
    got = lax.all_to_all(message, LEAF, 0, 0, tiled=True)
    bottleneck, d_queries, d_keyval, d_roots, pack = call(
        unpack_kernel, [(16, 512), (16, 512), (16, 1024), (4, 16, 128), (24, 3072)]
    )(got, rows, root_rows, cotangent)
    swap = lambda v: lax.ppermute(v, "co", [(0, 1), (1, 0)])
    output, upper = call(upper_kernel, [(16, 512), (512, 1024)], (), True)(
        core, coarse, bottleneck, w_out, pack, swap(pack)
    )
    upper, *far = lax.optimization_barrier((upper, *group_swaps(d_roots)))
    upper = lax.all_to_all(upper.reshape(64, 8, 1024), CHIPS, 0, 0, tiled=True)
    keep, send = call(
        backward_kernel,
        [(64, 88, 128), (64, 88, 128)],
        [(4, 16, 128), (3, 64, 128), (1024, 384), (1024, 128)],
        True,
        pl.CostEstimate(flops=12_000_000_000, bytes_accessed=20_000_000, transcendentals=0),
    )(
        group, d_roots, *far, d_queries, d_keyval, rows, coarse, cotangent,
        gain_coarse, w_query, w_keyval, w_three, w_two, w_one, w_out_leaf, w_qkv, gain_leaf,
        *saved,
    )
    send, upper = lax.optimization_barrier((send, upper))
    upper = spread(jnp.sum(upper, axis=0), CHIPS, 64).reshape(512, 1024)
    late, upper = lax.optimization_barrier((keep + swap(send), upper))
    late = jnp.sum(lax.all_to_all(late, CHIPS, 0, 0, tiled=True), axis=0)
    late = spread(late, CHIPS, 64)
    upper = call(assemble_upper_kernel, [(512, 512), (512, 1024), (512, 512)], (), True)(
        core, upper, swap(upper)
    )
    late, *upper = lax.optimization_barrier((late, *upper))
    gain_leaf, gain_coarse, *rest = call(
        assemble_kernel,
        [(128,), (512,), (128, 384), (128, 128), (512, 256), (1024, 384), (1536, 512)],
        (),
        True,
    )(core, late, swap(late))
    return (output, gain_leaf, *rest, gain_coarse, *upper)


def solution(mesh):
    fine = Mesh(mesh.devices.reshape(2, 2, 2, 4, 4), ALL)
    cut = P(ALL, None)
    return jax.shard_map(
        shards,
        mesh=fine,
        in_specs=(cut, cut) + (P(),) * 10 + (cut,),
        out_specs=(cut,) + (P(),) * 10,
        check_vma=False,
    )
```

```python
import jax
import jax.numpy as jnp
from jax import lax
from jax.experimental import pallas as pl
from jax.experimental.pallas import tpu as pltpu
from jax.sharding import Mesh
from jax.sharding import PartitionSpec as P

GRP = ("zh", "co")
LEAF = ("zl", "y", "x")
ALL = GRP + LEAF
CHIPS = ("zh",) + LEAF
N_LEAF = 32
HEADS = 16
SCALE = 32 ** (-0.5)
F32 = jnp.float32


def split(value):
    high = value.astype(jnp.bfloat16)
    return high, (value - high.astype(F32)).astype(jnp.bfloat16)


def dot3(left, right, dims):
    left_high, left_low = split(left)
    right_high, right_low = split(right)
    go = lambda a, b: lax.dot_general(a, b, (dims, ((), ())), preferred_element_type=F32)
    return go(left_high, right_high) + (go(left_high, right_low) + go(left_low, right_high))


def mm(left, right):
    return dot3(left, right, ((1,), (0,)))


def mm_t(left, right):
    return dot3(left, right, ((1,), (1,)))


def t_mm(left, right):
    return dot3(left, right, ((0,), (0,)))


def full(left, right, dims):
    return lax.dot_general(
        left, right, (dims, ((), ())), precision=lax.Precision.HIGHEST, preferred_element_type=F32
    )


def mm6(left, right):
    return full(left, right, ((1,), (0,)))


def mm6_t(left, right):
    return full(left, right, ((1,), (1,)))


def t_mm6(left, right):
    return full(left, right, ((0,), (0,)))


def lanes(at):
    lane = lax.broadcasted_iota(jnp.int32, (1, 128), 1)
    return ((lane >= 32 * at) & (lane < 32 * at + 32)).astype(F32)


def turn(value, by):
    by = by % 128
    return value if by == 0 else pltpu.roll(value, by, 1)


def inverse_rms(values):
    return lax.rsqrt(jnp.mean(values * values, axis=-1, keepdims=True) + 1e-06)


def sigmoid(pre):
    return 1.0 / (1.0 + jnp.exp(-pre))


def softmax(scores):
    weights = jnp.exp(scores - jnp.max(scores, axis=-1, keepdims=True))
    return weights / jnp.sum(weights, axis=-1, keepdims=True)


def four(value):
    return jnp.concatenate([value * lanes(h) for h in range(4)], axis=0)


def slot_one(rows, at):
    return rows.reshape(8, 4, 32, rows.shape[-1])[:, at].reshape(256, rows.shape[-1])


def slot_two(rows, at):
    return rows.reshape(8, 4, 8, rows.shape[-1])[:, at].reshape(64, rows.shape[-1])


def stride_get(ref, at, stride):
    blocks = [ref[j, pl.ds(at, 8, stride=stride), :] for j in range(ref.shape[0])]
    return jnp.concatenate(blocks, axis=1)


def stride_put(ref, at, stride, value):
    for j in range(ref.shape[0]):
        ref[j, pl.ds(at, 8, stride=stride), :] = value[:, 128 * j : 128 * j + 128]


def put_blocks(ref, value):
    for j in range(ref.shape[0]):
        ref[j] = value[:, 128 * j : 128 * j + 128]


def get_blocks(ref):
    return jnp.concatenate([ref[j] for j in range(ref.shape[0])], axis=1)


def slot_three(ref, at):
    return jnp.concatenate([stride_get(ref, 2 * at + a, 8) for a in range(2)], axis=0)


def forward_kernel(
    order, features, gain_leaf, w_qkv, w_out_leaf, gain_coarse, cotangent,
    far_one, far_two, far_three, far_query, far_keyval, far_out,
    unit, packed, weights, attended, mixed, pre_one, pre_two, two, coarse, rows, message, roots,
    ordered, natural, w_one, w_two, w_three, w_query, w_keyval, w_out, arrived,
):
    pairs = (
        (far_one, w_one), (far_two, w_two), (far_three, w_three),
        (far_query, w_query), (far_keyval, w_keyval), (far_out, w_out),
    )
    copies = [pltpu.make_async_copy(*pair, arrived.at[i]) for i, pair in enumerate(pairs)]
    for copy in copies:
        copy.start()
    wait = lambda i: copies[i].wait()

    def fetch(step, carry):
        ball, rest = step // 16, step % 16
        base = ball * 128 + (rest % 4) * 4 + rest // 4
        for d2 in range(4):
            for a in range(2):
                source = order[0, base + 64 * a + 16 * d2]
                ordered[pl.ds(step * 8 + 2 * d2 + a, 1), :] = features[pl.ds(source, 1), :]
        return carry

    lax.fori_loop(0, 128, fetch, 0, unroll=8)
    unit[...] = ordered[...] * inverse_rms(ordered[...])
    packed[...] = mm6(unit[...] * gain_leaf[...], w_qkv[...])

    def ball(step, carry):
        at = pl.ds(step * 128, 128)
        values = packed[at, 256:]
        scores = mm_t(four(packed[at, :128] * SCALE), packed[at, 128:256])
        probs = softmax(scores)
        weights[pl.ds(step * 512, 512), :] = probs
        wide = jnp.concatenate([probs[128 * h : 128 * h + 128] for h in range(4)], axis=1)
        attended[at, :] = mm(wide, four(values))
        return carry

    lax.fori_loop(0, 8, ball, 0, unroll=8)
    joined = ordered[...] + mm6(attended[...], w_out_leaf[...])
    mixed[...] = joined
    wait(0)
    pre = mm6(jnp.concatenate([slot_one(joined, d) for d in range(4)], axis=1), w_one[...])
    pre_one[...] = pre
    one = pre * sigmoid(pre)
    wait(1)
    pre = mm6(jnp.concatenate([slot_two(one, d) for d in range(4)], axis=1), w_two[...])
    pre_two[...] = pre
    put_blocks(two, pre * sigmoid(pre))
    wait(2)
    top = mm6(jnp.concatenate([slot_three(two, d) for d in range(4)], axis=1), w_three[...])
    for a in range(2):
        stride_put(natural, a, 2, top[8 * a : 8 * a + 8])
    top = get_blocks(natural)
    coarse[...] = top
    means = jnp.concatenate(
        [jnp.mean(top[8 * r : 8 * r + 8], axis=0, keepdims=True) for r in range(2)]
        + [jnp.zeros((6, 512), F32)],
        axis=0,
    )
    normed = jnp.concatenate([top * inverse_rms(top), means * inverse_rms(means)], axis=0)
    normed = normed * gain_coarse[...]
    rows[...] = normed
    for i in range(3, 6):
        wait(i)
    queries = mm6(normed[:16], w_query[...])
    keyval = mm6(normed, w_keyval[...])
    d_bottleneck = mm6_t(cotangent[...], w_out[...])
    parts = (queries, keyval[:16, :512], keyval[:16, 512:], d_bottleneck)
    for h in range(HEADS):
        block = slice(128 * (h // 4), 128 * (h // 4) + 128)
        message[h] = sum(
            turn(part[:, block], 32 * (c - h % 4)) * lanes(c) for c, part in enumerate(parts)
        )
    for j in range(8):
        roots[2 * j : 2 * j + 2, :] = keyval[16:18, 128 * j : 128 * j + 128]
    for j in range(4):
        roots[16 + 2 * j : 18 + 2 * j, :] = normed[16:18, 128 * j : 128 * j + 128]


def message_kernel(group, main, roots, one, two, three, message, root_rows, sorted_roots):
    for k, part in enumerate((roots, one, two, three)):
        sorted_roots[group[0] ^ k] = part[...]
    roots = sorted_roots
    block = lambda j: roots[:, 2 * j : 2 * j + 2, :].reshape(8, 128)
    for h in range(HEADS):
        side = turn(block(h // 4), -32 * (h % 4)) * lanes(0)
        side = side + turn(block(4 + h // 4), 32 - 32 * (h % 4)) * lanes(1)
        for half in range(2):
            message[2 * h + half, :16, :] = main[h]
            message[2 * h + half, 16:, :] = side
    for j in range(4):
        root_rows[:, 128 * j : 128 * j + 128] = block(8 + j)


def attend_kernel(half, got, message):
    at = pl.multiple_of(half[0] * 8, 8)
    mine = got[:, pl.ds(at, 8), :].reshape(256, 128)
    every = got[:, :16, :].reshape(512, 128)
    away = got[:, 16:, :].reshape(256, 128)
    queries = mine * lanes(0) * SCALE
    d_out = mine * lanes(3)

    def scores_of(keys, values):
        probs = softmax(mm6_t(queries, keys))
        d_probs = mm6_t(d_out, values)
        d_scores = probs * (d_probs - jnp.sum(probs * d_probs, axis=-1, keepdims=True))
        return probs, d_scores * SCALE

    probs, d_scores = scores_of(turn(every, -32), turn(every, 32))
    front = mm6(probs, turn(every, -64) * lanes(0)) + mm6(d_scores, every * lanes(1))
    back = t_mm6(d_scores, turn(mine, 64) * lanes(2)) + t_mm6(probs, d_out)
    probs, d_scores = scores_of(away, turn(away, 64))
    front = front + mm6(probs, turn(away, -32) * lanes(0))
    front = front + mm6(d_scores, turn(away, 32) * lanes(1))
    side = t_mm6(d_scores, mine * lanes(0)) + t_mm6(probs, turn(mine, 64) * lanes(1))
    message[:, :16, :] = back.reshape(N_LEAF, 16, 128)
    message[:, pl.ds(at, 8), :] = message[:, pl.ds(at, 8), :] + front.reshape(N_LEAF, 8, 128)
    message[:, 16:, :] = side.reshape(N_LEAF, 8, 128)


def unpack_kernel(got, rows, root_rows, cotangent, bottleneck, d_queries, d_keyval, d_roots, pack):
    pack[16:, :1024] = jnp.zeros((8, 1024), F32)
    pack[16:, 2560:] = jnp.zeros((8, 512), F32)
    pack[:16, 2048:2560] = rows[:16, :]
    pack[16:, 2048:2560] = root_rows[...]
    pack[:16, 2560:] = cotangent[...]
    for block in range(4):
        heads = [got[2 * h] + got[2 * h + 1] for h in range(4 * block, 4 * block + 4)]
        pick = lambda c, rows: sum(
            turn(heads[k][rows], 32 * (k - c)) * lanes(k) for k in range(4)
        )
        own, far = slice(0, 16), slice(16, 24)
        for c, ref in enumerate((bottleneck, d_queries, d_keyval, d_keyval)):
            at = 128 * block + (512 if c == 3 else 0)
            value = pick(c, own)
            ref[:, at : at + 128] = value
            pack[:16, 512 * c + 128 * block : 512 * c + 128 * block + 128] = value
        for c in range(2):
            value = pick(c, far)
            at = 8 * c + 2 * block
            d_roots[:, at : at + 2, :] = value.reshape(4, 2, 128)
            at = 1024 + 512 * c + 128 * block
            pack[16:, at : at + 128] = value


def upper_kernel(core, mine, other, grads):
    both = lambda at, width: jnp.concatenate(
        [mine[:, pl.ds(at, width)], other[:, pl.ds(at, width)]], axis=0
    )
    half = lambda at, width: both(pl.multiple_of(at + core[0] * width, 128), width)
    normed = both(2048, 512)
    grads[:, :256] = t_mm(both(0, 512), half(2560, 256))
    grads[:, 256:512] = t_mm(normed, half(512, 256))
    grads[:, 512:] = t_mm(normed, half(1024, 512))


def assemble_upper_kernel(core, mine, other, grad_query, grad_keyval, grad_out):
    def fill(half, source):
        grad_out[:, 256 * half : 256 * half + 256] = source[:, :256]
        grad_query[:, 256 * half : 256 * half + 256] = source[:, 256:512]
        grad_keyval[:, 512 * half : 512 * half + 512] = source[:, 512:]

    for half in range(2):

        @pl.when(core[0] == half)
        def _():
            fill(half, mine)
            fill(1 - half, other)


def rms_backward(d_normed, values, gain):
    scale = inverse_rms(values)
    unit = values * scale
    d_unit = d_normed * gain
    d_values = scale * (d_unit - unit * jnp.mean(d_unit * unit, axis=-1, keepdims=True))
    return d_values, jnp.sum(d_normed * unit, axis=0, keepdims=True)


def backward_kernel(
    group, d_roots, roots_one, roots_two, roots_three, bottleneck, w_out, d_queries, d_keyval, rows, coarse, cotangent, gain_coarse, w_query, w_keyval,
    w_three, w_two, w_one, w_out_leaf, w_qkv, gain_leaf,
    unit, packed, weights, attended, mixed, pre_one, pre_two, two,
    output, keep, send,
    d_coarse, d_two, d_packed, d_attended,
):
    def put(half, chips, at, value):
        chips, at = pl.ds(*chips), pl.ds(*at)

        @pl.when(core == half)
        def _():
            keep[chips, at, :] = value

        @pl.when(core != half)
        def _():
            send[chips, at, :] = value

    core = group[0] % 2
    output[...] = coarse[...] + mm6(bottleneck[...], w_out[...])
    far = sum(ref[group[0]] for ref in (d_roots, roots_one, roots_two, roots_three))
    far = jnp.concatenate([far[2 * j : 2 * j + 2] for j in range(8)], axis=1)
    d_kv = jnp.concatenate([d_keyval[...], far, jnp.zeros((6, 1024), F32)], axis=0)
    d_rows = mm6_t(d_kv, w_keyval[...])
    top = coarse[...]
    d_top, gain_a = rms_backward(
        d_rows[:16] + mm6_t(d_queries[...], w_query[...]), top, gain_coarse[...]
    )
    means = jnp.concatenate(
        [jnp.mean(top[8 * r : 8 * r + 8], axis=0, keepdims=True) for r in range(2)], axis=0
    )
    d_means, gain_b = rms_backward(d_rows[16:18], means, gain_coarse[...])
    d_means = d_means * 0.125
    d_means = jnp.concatenate(
        [jnp.broadcast_to(d_means[r : r + 1], (8, 512)) for r in range(2)], axis=0
    )
    put_blocks(d_coarse, cotangent[...] + d_top + d_means)
    gain_c = gain_a + gain_b

    d_top = jnp.concatenate([stride_get(d_coarse, a, 2) for a in range(2)], axis=0)
    for d in range(4):
        at = slice(384 * d, 384 * d + 384)
        grad = t_mm(slot_three(two, d), d_top)
        for i in range(4):
            block = grad[:, 128 * i : 128 * i + 128].reshape(16, 24, 128)
            put(i // 2, (16 * d, 16), (24 * (i % 2), 24), block)
        part = mm6_t(d_top, w_three[at, :])
        for a in range(2):
            stride_put(d_two, 2 * d + a, 8, part[8 * a : 8 * a + 8])
    pre = pre_two[...]
    gate = sigmoid(pre)
    d_pre = get_blocks(d_two) * (gate * (1.0 + pre * (1.0 - gate)))
    pre = pre_one[...]
    gate = sigmoid(pre)
    one = pre * gate
    parts = []
    for d in range(4):
        at = slice(256 * d, 256 * d + 256)
        grad = t_mm(slot_two(one, d), d_pre)
        for i in range(3):
            block = grad[:, 128 * i : 128 * i + 128].reshape(32, 8, 128)
            put(d // 2, (32 * (d % 2), 32), (48 + 8 * i, 8), block)
        parts.append(mm6_t(d_pre, w_two[at, :]).reshape(8, 1, 8, 256))
    d_one = jnp.concatenate(parts, axis=1).reshape(256, 256)
    d_pre = d_one * (gate * (1.0 + pre * (1.0 - gate)))
    joined = mixed[...]
    parts = []
    for d in range(4):
        at = slice(128 * d, 128 * d + 128)
        grad = t_mm(slot_one(joined, d), d_pre)
        for i in range(2):
            put(i, (16 * d, 16), (72, 8), grad[:, 128 * i : 128 * i + 128].reshape(16, 8, 128))
        parts.append(mm_t(d_pre, w_one[at, :]).reshape(8, 1, 32, 128))
    d_mixed = jnp.concatenate(parts, axis=1).reshape(1024, 128)
    grad_out_leaf = t_mm(attended[...], d_mixed)
    d_attended[...] = mm_t(d_mixed, w_out_leaf[...])

    def ball(step, carry):
        at = pl.ds(step * 128, 128)
        probs = weights[pl.ds(step * 512, 512), :]
        d_out = four(d_attended[at, :])
        d_probs = mm6_t(d_out, packed[at, 256:])
        d_scores = probs * (d_probs - jnp.sum(probs * d_probs, axis=-1, keepdims=True)) * SCALE
        wide = jnp.concatenate([d_scores[128 * h : 128 * h + 128] for h in range(4)], axis=1)
        d_packed[at, :128] = mm(wide, four(packed[at, 128:256]))
        d_packed[at, 128:256] = t_mm(d_scores, four(packed[at, :128]))
        d_packed[at, 256:] = t_mm(probs, d_out)
        return carry

    lax.fori_loop(0, 8, ball, 0, unroll=4)
    grad_qkv = t_mm(unit[...] * gain_leaf[...], d_packed[...])
    blocks = [grad_qkv[:, 128 * i : 128 * i + 128] for i in range(3)] + [grad_out_leaf]
    for i, block in enumerate(blocks):
        put(i // 2, (16 * (i % 2), 16), (80, 8), block.reshape(16, 8, 128))
    d_normed = mm_t(d_packed[...], w_qkv[...])
    gains = jnp.concatenate(
        [jnp.sum(d_normed * unit[...], axis=0, keepdims=True)]
        + [gain_c[:, 128 * j : 128 * j + 128] for j in range(4)]
        + [jnp.zeros((3, 128), F32)],
        axis=0,
    )
    put(0, (32, 1), (80, 8), gains.reshape(1, 8, 128))
    put(0, (33, 31), (80, 8), jnp.zeros((31, 8, 128), F32))
    put(1, (32, 32), (80, 8), jnp.zeros((32, 8, 128), F32))


def assemble_kernel(
    core, mine, other,
    gain_leaf, gain_coarse, grad_qkv, grad_out_leaf, grad_one, grad_two, grad_three,
):
    def fill(half, source):
        for i in range(2):
            at = 256 * half + 128 * i
            grad_three[:, at : at + 128] = source[:, 24 * i : 24 * i + 24, :].reshape(1536, 128)
        for i in range(3):
            block = source[:, 48 + 8 * i : 56 + 8 * i, :].reshape(512, 128)
            grad_two[512 * half : 512 * half + 512, 128 * i : 128 * i + 128] = block
        grad_one[:, 128 * half : 128 * half + 128] = source[:, 72:80, :].reshape(512, 128)
        first = source[0:16, 80:88, :].reshape(128, 128)
        second = source[16:32, 80:88, :].reshape(128, 128)
        if half == 0:
            grad_qkv[:, :128] = first
            grad_qkv[:, 128:256] = second
            gain_leaf[...] = source[32, 80, :]
            for i in range(4):
                gain_coarse[128 * i : 128 * i + 128] = source[32, 81 + i, :]
        else:
            grad_qkv[:, 256:] = first
            grad_out_leaf[...] = second

    for half in range(2):

        @pl.when(core[0] == half)
        def _():
            fill(half, mine)
            fill(1 - half, other)


def call(kernel, outs, scratch=(), smem_first=False, cost=None, far=0):
    shapes = [jax.ShapeDtypeStruct(shape, F32) for shape in outs]

    rooms = [pltpu.VMEM(shape, F32) for shape in scratch]

    def run(*args):
        specs = [pl.BlockSpec(memory_space=pltpu.VMEM)] * len(args)
        if smem_first:
            specs[0] = pl.BlockSpec(memory_space=pltpu.SMEM)
        if far:
            specs[-far:] = [pl.BlockSpec(memory_space=pl.ANY)] * far
            rooms.append(pltpu.SemaphoreType.DMA((far,)))
        return pl.pallas_call(
            kernel,
            out_shape=shapes,
            in_specs=specs,
            out_specs=[pl.BlockSpec(memory_space=pltpu.VMEM)] * len(shapes),
            scratch_shapes=rooms,
            cost_estimate=cost,
            compiler_params=pltpu.CompilerParams(vmem_limit_bytes=56 * 2**20),
        )(*args)

    return run


def group_swaps(value):
    return [lax.ppermute(value, GRP, [(i, i ^ k) for i in range(4)]) for k in range(1, 4)]


def spread(value, axes, parts):
    wide = jnp.broadcast_to(value[None], (parts,) + value.shape)
    return lax.all_to_all(wide, axes, 0, 0, tiled=True)


def shards(
    features, tree_order, gain_leaf, w_qkv, w_out_leaf, w_one, w_two, w_three, gain_coarse,
    w_query, w_keyval, w_out, cotangent,
):
    half = (lax.axis_index("x") % 2).astype(jnp.int32).reshape(1)
    group = lax.axis_index(GRP).astype(jnp.int32).reshape(1)
    core = lax.axis_index("co").astype(jnp.int32).reshape(1)
    gain_leaf = gain_leaf.reshape(1, 128)
    gain_coarse = gain_coarse.reshape(1, 512)
    saved_shapes = [
        (1024, 128), (1024, 384), (4096, 128), (1024, 128), (1024, 128), (256, 256), (64, 384),
        (3, 64, 128),
    ]
    *saved, coarse, rows, main, roots = call(
        forward_kernel,
        saved_shapes + [(16, 512), (24, 512), (HEADS, 16, 128), (24, 128)],
        [(1024, 128), (4, 16, 128), (512, 256), (1024, 384), (1536, 512), (512, 512), (512, 1024),
         (512, 512)],
        True,
        far=6,
    )(
        tree_order, features, gain_leaf, w_qkv, w_out_leaf, gain_coarse, cotangent,
        w_one, w_two, w_three, w_query, w_keyval, w_out,
    )
    message, root_rows = call(
        message_kernel, [(N_LEAF, 24, 128), (8, 512)], [(4, 24, 128)], True
    )(group, main, roots, *group_swaps(roots))
    got = lax.all_to_all(message, LEAF, 0, 0, tiled=True)
    message = call(attend_kernel, [(N_LEAF, 24, 128)], (), True)(half, got)[0]
    got = lax.all_to_all(message, LEAF, 0, 0, tiled=True)
    bottleneck, d_queries, d_keyval, d_roots, pack = call(
        unpack_kernel, [(16, 512), (16, 512), (16, 1024), (4, 16, 128), (24, 3072)]
    )(got, rows, root_rows, cotangent)
    swap = lambda v: lax.ppermute(v, "co", [(0, 1), (1, 0)])
    upper = call(upper_kernel, [(512, 1024)], (), True)(core, pack, swap(pack))[0]
    upper, *far = lax.optimization_barrier((upper, *group_swaps(d_roots)))
    upper = lax.all_to_all(upper.reshape(64, 8, 1024), CHIPS, 0, 0, tiled=True)
    output, keep, send = call(
        backward_kernel,
        [(16, 512), (64, 88, 128), (64, 88, 128)],
        [(4, 16, 128), (3, 64, 128), (1024, 384), (1024, 128)],
        True,
        pl.CostEstimate(flops=12_000_000_000, bytes_accessed=20_000_000, transcendentals=0),
    )(
        group, d_roots, *far, bottleneck, w_out, d_queries, d_keyval, rows, coarse, cotangent,
        gain_coarse, w_query, w_keyval, w_three, w_two, w_one, w_out_leaf, w_qkv, gain_leaf,
        *saved,
    )
    send, upper = lax.optimization_barrier((send, upper))
    upper = spread(jnp.sum(upper, axis=0), CHIPS, 64).reshape(512, 1024)
    late, upper = lax.optimization_barrier((keep + swap(send), upper))
    late = jnp.sum(lax.all_to_all(late, CHIPS, 0, 0, tiled=True), axis=0)
    late = spread(late, CHIPS, 64)
    upper = call(assemble_upper_kernel, [(512, 512), (512, 1024), (512, 512)], (), True)(
        core, upper, swap(upper)
    )
    late, *upper = lax.optimization_barrier((late, *upper))
    gain_leaf, gain_coarse, *rest = call(
        assemble_kernel,
        [(128,), (512,), (128, 384), (128, 128), (512, 256), (1024, 384), (1536, 512)],
        (),
        True,
    )(core, late, swap(late))
    return (output, gain_leaf, *rest, gain_coarse, *upper)


def solution(mesh):
    fine = Mesh(mesh.devices.reshape(2, 2, 2, 4, 4), ALL)
    cut = P(ALL, None)
    return jax.shard_map(
        shards,
        mesh=fine,
        in_specs=(cut, cut) + (P(),) * 10 + (cut,),
        out_specs=(cut,) + (P(),) * 10,
        check_vma=False,
    )
```

```python
import jax
import jax.numpy as jnp
from jax import lax
from jax.experimental import pallas as pl
from jax.experimental.pallas import tpu as pltpu
from jax.sharding import Mesh
from jax.sharding import PartitionSpec as P

GRP = ("zh", "co")
LEAF = ("zl", "y", "x")
ALL = GRP + LEAF
CHIPS = ("zh",) + LEAF
N_LEAF = 32
HEADS = 16
SCALE = 32 ** (-0.5)
F32 = jnp.float32


def split(value):
    high = value.astype(jnp.bfloat16)
    return high, (value - high.astype(F32)).astype(jnp.bfloat16)


def dot3(left, right, dims):
    left_high, left_low = split(left)
    right_high, right_low = split(right)
    go = lambda a, b: lax.dot_general(a, b, (dims, ((), ())), preferred_element_type=F32)
    return go(left_high, right_high) + (go(left_high, right_low) + go(left_low, right_high))


def mm(left, right):
    return dot3(left, right, ((1,), (0,)))


def mm_t(left, right):
    return dot3(left, right, ((1,), (1,)))


def t_mm(left, right):
    return dot3(left, right, ((0,), (0,)))


def full(left, right, dims):
    return lax.dot_general(
        left, right, (dims, ((), ())), precision=lax.Precision.HIGHEST, preferred_element_type=F32
    )


def mm6(left, right):
    return full(left, right, ((1,), (0,)))


def mm6_t(left, right):
    return full(left, right, ((1,), (1,)))


def t_mm6(left, right):
    return full(left, right, ((0,), (0,)))


def lanes(at):
    lane = lax.broadcasted_iota(jnp.int32, (1, 128), 1)
    return ((lane >= 32 * at) & (lane < 32 * at + 32)).astype(F32)


def turn(value, by):
    by = by % 128
    return value if by == 0 else pltpu.roll(value, by, 1)


def inverse_rms(values):
    return lax.rsqrt(jnp.mean(values * values, axis=-1, keepdims=True) + 1e-06)


def sigmoid(pre):
    return 1.0 / (1.0 + jnp.exp(-pre))


def softmax(scores):
    weights = jnp.exp(scores - jnp.max(scores, axis=-1, keepdims=True))
    return weights / jnp.sum(weights, axis=-1, keepdims=True)


def four(value):
    return jnp.concatenate([value * lanes(h) for h in range(4)], axis=0)


def slot_one(rows, at):
    return rows.reshape(8, 4, 32, rows.shape[-1])[:, at].reshape(256, rows.shape[-1])


def slot_two(rows, at):
    return rows.reshape(8, 4, 8, rows.shape[-1])[:, at].reshape(64, rows.shape[-1])


def stride_get(ref, at, stride):
    blocks = [ref[j, pl.ds(at, 8, stride=stride), :] for j in range(ref.shape[0])]
    return jnp.concatenate(blocks, axis=1)


def stride_put(ref, at, stride, value):
    for j in range(ref.shape[0]):
        ref[j, pl.ds(at, 8, stride=stride), :] = value[:, 128 * j : 128 * j + 128]


def put_blocks(ref, value):
    for j in range(ref.shape[0]):
        ref[j] = value[:, 128 * j : 128 * j + 128]


def get_blocks(ref):
    return jnp.concatenate([ref[j] for j in range(ref.shape[0])], axis=1)


def slot_three(ref, at):
    return jnp.concatenate([stride_get(ref, 2 * at + a, 8) for a in range(2)], axis=0)


def forward_kernel(
    order, features, gain_leaf, w_qkv, w_out_leaf, gain_coarse, cotangent,
    far_one, far_two, far_three, far_query, far_keyval, far_out,
    unit, packed, weights, attended, mixed, pre_one, pre_two, two, coarse, rows, message, roots,
    ordered, natural, w_one, w_two, w_three, w_query, w_keyval, w_out, arrived,
):
    pairs = (
        (far_one, w_one), (far_two, w_two), (far_three, w_three),
        (far_query, w_query), (far_keyval, w_keyval), (far_out, w_out),
    )
    copies = [pltpu.make_async_copy(*pair, arrived.at[i]) for i, pair in enumerate(pairs)]
    for copy in copies:
        copy.start()
    wait = lambda i: copies[i].wait()

    def fetch(step, carry):
        ball, rest = step // 16, step % 16
        base = ball * 128 + (rest % 4) * 4 + rest // 4
        for d2 in range(4):
            for a in range(2):
                source = order[0, base + 64 * a + 16 * d2]
                ordered[pl.ds(step * 8 + 2 * d2 + a, 1), :] = features[pl.ds(source, 1), :]
        return carry

    lax.fori_loop(0, 128, fetch, 0, unroll=8)
    unit[...] = ordered[...] * inverse_rms(ordered[...])
    packed[...] = mm6(unit[...] * gain_leaf[...], w_qkv[...])

    def ball(step, carry):
        at = pl.ds(step * 128, 128)
        values = packed[at, 256:]
        scores = mm_t(four(packed[at, :128] * SCALE), packed[at, 128:256])
        probs = softmax(scores)
        weights[pl.ds(step * 512, 512), :] = probs
        wide = jnp.concatenate([probs[128 * h : 128 * h + 128] for h in range(4)], axis=1)
        attended[at, :] = mm(wide, four(values))
        return carry

    lax.fori_loop(0, 8, ball, 0, unroll=8)
    joined = ordered[...] + mm6(attended[...], w_out_leaf[...])
    mixed[...] = joined
    wait(0)
    pre = mm6(jnp.concatenate([slot_one(joined, d) for d in range(4)], axis=1), w_one[...])
    pre_one[...] = pre
    one = pre * sigmoid(pre)
    wait(1)
    pre = mm6(jnp.concatenate([slot_two(one, d) for d in range(4)], axis=1), w_two[...])
    pre_two[...] = pre
    put_blocks(two, pre * sigmoid(pre))
    wait(2)
    top = mm6(jnp.concatenate([slot_three(two, d) for d in range(4)], axis=1), w_three[...])
    for a in range(2):
        stride_put(natural, a, 2, top[8 * a : 8 * a + 8])
    top = get_blocks(natural)
    coarse[...] = top
    means = jnp.concatenate(
        [jnp.mean(top[8 * r : 8 * r + 8], axis=0, keepdims=True) for r in range(2)]
        + [jnp.zeros((6, 512), F32)],
        axis=0,
    )
    normed = jnp.concatenate([top * inverse_rms(top), means * inverse_rms(means)], axis=0)
    normed = normed * gain_coarse[...]
    rows[...] = normed
    for i in range(3, 6):
        wait(i)
    queries = mm6(normed[:16], w_query[...])
    keyval = mm6(normed, w_keyval[...])
    d_bottleneck = mm6_t(cotangent[...], w_out[...])
    parts = (queries, keyval[:16, :512], keyval[:16, 512:], d_bottleneck)
    for h in range(HEADS):
        block = slice(128 * (h // 4), 128 * (h // 4) + 128)
        message[h] = sum(
            turn(part[:, block], 32 * (c - h % 4)) * lanes(c) for c, part in enumerate(parts)
        )
    for j in range(8):
        roots[2 * j : 2 * j + 2, :] = keyval[16:18, 128 * j : 128 * j + 128]
    for j in range(4):
        roots[16 + 2 * j : 18 + 2 * j, :] = normed[16:18, 128 * j : 128 * j + 128]


def message_kernel(group, main, roots, one, two, three, message, root_rows, sorted_roots):
    for k, part in enumerate((roots, one, two, three)):
        sorted_roots[group[0] ^ k] = part[...]
    roots = sorted_roots
    block = lambda j: roots[:, 2 * j : 2 * j + 2, :].reshape(8, 128)
    for h in range(HEADS):
        side = turn(block(h // 4), -32 * (h % 4)) * lanes(0)
        side = side + turn(block(4 + h // 4), 32 - 32 * (h % 4)) * lanes(1)
        for half in range(2):
            message[2 * h + half, :16, :] = main[h]
            message[2 * h + half, 16:, :] = side
    for j in range(4):
        root_rows[:, 128 * j : 128 * j + 128] = block(8 + j)


def attend_kernel(half, got, message):
    at = pl.multiple_of(half[0] * 8, 8)
    mine = got[:, pl.ds(at, 8), :].reshape(256, 128)
    every = got[:, :16, :].reshape(512, 128)
    away = got[:, 16:, :].reshape(256, 128)
    queries = mine * lanes(0) * SCALE
    d_out = mine * lanes(3)

    def scores_of(keys, values):
        probs = softmax(mm6_t(queries, keys))
        d_probs = mm6_t(d_out, values)
        d_scores = probs * (d_probs - jnp.sum(probs * d_probs, axis=-1, keepdims=True))
        return probs, d_scores * SCALE

    probs, d_scores = scores_of(turn(every, -32), turn(every, 32))
    front = mm(probs, turn(every, -64) * lanes(0)) + mm(d_scores, every * lanes(1))
    back = t_mm(d_scores, turn(mine, 64) * lanes(2)) + t_mm(probs, d_out)
    probs, d_scores = scores_of(away, turn(away, 64))
    front = front + mm(probs, turn(away, -32) * lanes(0))
    front = front + mm(d_scores, turn(away, 32) * lanes(1))
    side = t_mm(d_scores, mine * lanes(0)) + t_mm(probs, turn(mine, 64) * lanes(1))
    message[:, :16, :] = back.reshape(N_LEAF, 16, 128)
    message[:, pl.ds(at, 8), :] = message[:, pl.ds(at, 8), :] + front.reshape(N_LEAF, 8, 128)
    message[:, 16:, :] = side.reshape(N_LEAF, 8, 128)


def unpack_kernel(got, rows, root_rows, cotangent, bottleneck, d_queries, d_keyval, d_roots, pack):
    pack[16:, :1024] = jnp.zeros((8, 1024), F32)
    pack[16:, 2560:] = jnp.zeros((8, 512), F32)
    pack[:16, 2048:2560] = rows[:16, :]
    pack[16:, 2048:2560] = root_rows[...]
    pack[:16, 2560:] = cotangent[...]
    for block in range(4):
        heads = [got[2 * h] + got[2 * h + 1] for h in range(4 * block, 4 * block + 4)]
        pick = lambda c, rows: sum(
            turn(heads[k][rows], 32 * (k - c)) * lanes(k) for k in range(4)
        )
        own, far = slice(0, 16), slice(16, 24)
        for c, ref in enumerate((bottleneck, d_queries, d_keyval, d_keyval)):
            at = 128 * block + (512 if c == 3 else 0)
            value = pick(c, own)
            ref[:, at : at + 128] = value
            pack[:16, 512 * c + 128 * block : 512 * c + 128 * block + 128] = value
        for c in range(2):
            value = pick(c, far)
            at = 8 * c + 2 * block
            d_roots[:, at : at + 2, :] = value.reshape(4, 2, 128)
            at = 1024 + 512 * c + 128 * block
            pack[16:, at : at + 128] = value


def upper_kernel(core, mine, other, grads):
    both = lambda at, width: jnp.concatenate(
        [mine[:, pl.ds(at, width)], other[:, pl.ds(at, width)]], axis=0
    )
    half = lambda at, width: both(pl.multiple_of(at + core[0] * width, 128), width)
    normed = both(2048, 512)
    grads[:, :256] = t_mm(both(0, 512), half(2560, 256))
    grads[:, 256:512] = t_mm(normed, half(512, 256))
    grads[:, 512:] = t_mm(normed, half(1024, 512))


def assemble_upper_kernel(core, mine, other, grad_query, grad_keyval, grad_out):
    def fill(half, source):
        grad_out[:, 256 * half : 256 * half + 256] = source[:, :256]
        grad_query[:, 256 * half : 256 * half + 256] = source[:, 256:512]
        grad_keyval[:, 512 * half : 512 * half + 512] = source[:, 512:]

    for half in range(2):

        @pl.when(core[0] == half)
        def _():
            fill(half, mine)
            fill(1 - half, other)


def rms_backward(d_normed, values, gain):
    scale = inverse_rms(values)
    unit = values * scale
    d_unit = d_normed * gain
    d_values = scale * (d_unit - unit * jnp.mean(d_unit * unit, axis=-1, keepdims=True))
    return d_values, jnp.sum(d_normed * unit, axis=0, keepdims=True)


def backward_kernel(
    group, d_roots, roots_one, roots_two, roots_three, bottleneck, w_out, d_queries, d_keyval, rows, coarse, cotangent, gain_coarse, w_query, w_keyval,
    w_three, w_two, w_one, w_out_leaf, w_qkv, gain_leaf,
    unit, packed, weights, attended, mixed, pre_one, pre_two, two,
    output, keep, send,
    d_coarse, d_two, d_packed, d_attended,
):
    def put(half, chips, at, value):
        chips, at = pl.ds(*chips), pl.ds(*at)

        @pl.when(core == half)
        def _():
            keep[chips, at, :] = value

        @pl.when(core != half)
        def _():
            send[chips, at, :] = value

    core = group[0] % 2
    output[...] = coarse[...] + mm6(bottleneck[...], w_out[...])
    far = sum(ref[group[0]] for ref in (d_roots, roots_one, roots_two, roots_three))
    far = jnp.concatenate([far[2 * j : 2 * j + 2] for j in range(8)], axis=1)
    d_kv = jnp.concatenate([d_keyval[...], far, jnp.zeros((6, 1024), F32)], axis=0)
    d_rows = mm6_t(d_kv, w_keyval[...])
    top = coarse[...]
    d_top, gain_a = rms_backward(
        d_rows[:16] + mm6_t(d_queries[...], w_query[...]), top, gain_coarse[...]
    )
    means = jnp.concatenate(
        [jnp.mean(top[8 * r : 8 * r + 8], axis=0, keepdims=True) for r in range(2)], axis=0
    )
    d_means, gain_b = rms_backward(d_rows[16:18], means, gain_coarse[...])
    d_means = d_means * 0.125
    d_means = jnp.concatenate(
        [jnp.broadcast_to(d_means[r : r + 1], (8, 512)) for r in range(2)], axis=0
    )
    put_blocks(d_coarse, cotangent[...] + d_top + d_means)
    gain_c = gain_a + gain_b

    d_top = jnp.concatenate([stride_get(d_coarse, a, 2) for a in range(2)], axis=0)
    for d in range(4):
        at = slice(384 * d, 384 * d + 384)
        grad = t_mm(slot_three(two, d), d_top)
        for i in range(4):
            block = grad[:, 128 * i : 128 * i + 128].reshape(16, 24, 128)
            put(i // 2, (16 * d, 16), (24 * (i % 2), 24), block)
        part = mm6_t(d_top, w_three[at, :])
        for a in range(2):
            stride_put(d_two, 2 * d + a, 8, part[8 * a : 8 * a + 8])
    pre = pre_two[...]
    gate = sigmoid(pre)
    d_pre = get_blocks(d_two) * (gate * (1.0 + pre * (1.0 - gate)))
    pre = pre_one[...]
    gate = sigmoid(pre)
    one = pre * gate
    parts = []
    for d in range(4):
        at = slice(256 * d, 256 * d + 256)
        grad = t_mm(slot_two(one, d), d_pre)
        for i in range(3):
            block = grad[:, 128 * i : 128 * i + 128].reshape(32, 8, 128)
            put(d // 2, (32 * (d % 2), 32), (48 + 8 * i, 8), block)
        parts.append(mm_t(d_pre, w_two[at, :]).reshape(8, 1, 8, 256))
    d_one = jnp.concatenate(parts, axis=1).reshape(256, 256)
    d_pre = d_one * (gate * (1.0 + pre * (1.0 - gate)))
    joined = mixed[...]
    parts = []
    for d in range(4):
        at = slice(128 * d, 128 * d + 128)
        grad = t_mm(slot_one(joined, d), d_pre)
        for i in range(2):
            put(i, (16 * d, 16), (72, 8), grad[:, 128 * i : 128 * i + 128].reshape(16, 8, 128))
        parts.append(mm_t(d_pre, w_one[at, :]).reshape(8, 1, 32, 128))
    d_mixed = jnp.concatenate(parts, axis=1).reshape(1024, 128)
    grad_out_leaf = t_mm(attended[...], d_mixed)
    d_attended[...] = mm_t(d_mixed, w_out_leaf[...])

    def ball(step, carry):
        at = pl.ds(step * 128, 128)
        probs = weights[pl.ds(step * 512, 512), :]
        d_out = four(d_attended[at, :])
        d_probs = mm6_t(d_out, packed[at, 256:])
        d_scores = probs * (d_probs - jnp.sum(probs * d_probs, axis=-1, keepdims=True)) * SCALE
        wide = jnp.concatenate([d_scores[128 * h : 128 * h + 128] for h in range(4)], axis=1)
        d_packed[at, :128] = mm(wide, four(packed[at, 128:256]))
        d_packed[at, 128:256] = t_mm(d_scores, four(packed[at, :128]))
        d_packed[at, 256:] = t_mm(probs, d_out)
        return carry

    lax.fori_loop(0, 8, ball, 0, unroll=4)
    grad_qkv = t_mm(unit[...] * gain_leaf[...], d_packed[...])
    blocks = [grad_qkv[:, 128 * i : 128 * i + 128] for i in range(3)] + [grad_out_leaf]
    for i, block in enumerate(blocks):
        put(i // 2, (16 * (i % 2), 16), (80, 8), block.reshape(16, 8, 128))
    d_normed = mm_t(d_packed[...], w_qkv[...])
    gains = jnp.concatenate(
        [jnp.sum(d_normed * unit[...], axis=0, keepdims=True)]
        + [gain_c[:, 128 * j : 128 * j + 128] for j in range(4)]
        + [jnp.zeros((3, 128), F32)],
        axis=0,
    )
    put(0, (32, 1), (80, 8), gains.reshape(1, 8, 128))
    put(0, (33, 31), (80, 8), jnp.zeros((31, 8, 128), F32))
    put(1, (32, 32), (80, 8), jnp.zeros((32, 8, 128), F32))


def assemble_kernel(
    core, far_mine, far_other,
    gain_leaf, gain_coarse, grad_qkv, grad_out_leaf, grad_one, grad_two, grad_three,
    mine, other, arrived,
):
    copies = []
    for at, rows in ((0, 24), (24, 24), (48, 24), (72, 16)):
        for far, near in ((far_mine, mine), (far_other, other)):
            at_rows = pl.ds(at, rows)
            copies.append(
                pltpu.make_async_copy(
                    far.at[:, at_rows, :], near.at[:, at_rows, :], arrived.at[len(copies)]
                )
            )
            copies[-1].start()

    def fill(half, source, step):
        if step < 2:
            at = 256 * half + 128 * step
            block = source[:, 24 * step : 24 * step + 24, :]
            grad_three[:, at : at + 128] = block.reshape(1536, 128)
        elif step == 2:
            for i in range(3):
                block = source[:, 48 + 8 * i : 56 + 8 * i, :].reshape(512, 128)
                grad_two[512 * half : 512 * half + 512, 128 * i : 128 * i + 128] = block
        else:
            grad_one[:, 128 * half : 128 * half + 128] = source[:, 72:80, :].reshape(512, 128)
            first = source[0:16, 80:88, :].reshape(128, 128)
            second = source[16:32, 80:88, :].reshape(128, 128)
            if half == 0:
                grad_qkv[:, :128] = first
                grad_qkv[:, 128:256] = second
                gain_leaf[...] = source[32, 80, :]
                for i in range(4):
                    gain_coarse[128 * i : 128 * i + 128] = source[32, 81 + i, :]
            else:
                grad_qkv[:, 256:] = first
                grad_out_leaf[...] = second

    for step in range(4):
        copies[2 * step].wait()
        copies[2 * step + 1].wait()
        for half in range(2):

            @pl.when(core[0] == half)
            def _():
                fill(half, mine, step)
                fill(1 - half, other, step)


def call(kernel, outs, scratch=(), smem_first=False, cost=None, far=0, copies=0):
    shapes = [jax.ShapeDtypeStruct(shape, F32) for shape in outs]

    rooms = [pltpu.VMEM(shape, F32) for shape in scratch]

    def run(*args):
        specs = [pl.BlockSpec(memory_space=pltpu.VMEM)] * len(args)
        if smem_first:
            specs[0] = pl.BlockSpec(memory_space=pltpu.SMEM)
        if far:
            specs[-far:] = [pl.BlockSpec(memory_space=pl.ANY)] * far
            rooms.append(pltpu.SemaphoreType.DMA((copies or far,)))
        return pl.pallas_call(
            kernel,
            out_shape=shapes,
            in_specs=specs,
            out_specs=[pl.BlockSpec(memory_space=pltpu.VMEM)] * len(shapes),
            scratch_shapes=rooms,
            cost_estimate=cost,
            compiler_params=pltpu.CompilerParams(vmem_limit_bytes=56 * 2**20),
        )(*args)

    return run


def group_swaps(value):
    return [lax.ppermute(value, GRP, [(i, i ^ k) for i in range(4)]) for k in range(1, 4)]


def spread(value, axes, parts):
    wide = jnp.broadcast_to(value[None], (parts,) + value.shape)
    return lax.all_to_all(wide, axes, 0, 0, tiled=True)


def shards(
    features, tree_order, gain_leaf, w_qkv, w_out_leaf, w_one, w_two, w_three, gain_coarse,
    w_query, w_keyval, w_out, cotangent,
):
    half = (lax.axis_index("x") % 2).astype(jnp.int32).reshape(1)
    group = lax.axis_index(GRP).astype(jnp.int32).reshape(1)
    core = lax.axis_index("co").astype(jnp.int32).reshape(1)
    gain_leaf = gain_leaf.reshape(1, 128)
    gain_coarse = gain_coarse.reshape(1, 512)
    saved_shapes = [
        (1024, 128), (1024, 384), (4096, 128), (1024, 128), (1024, 128), (256, 256), (64, 384),
        (3, 64, 128),
    ]
    *saved, coarse, rows, main, roots = call(
        forward_kernel,
        saved_shapes + [(16, 512), (24, 512), (HEADS, 16, 128), (24, 128)],
        [(1024, 128), (4, 16, 128), (512, 256), (1024, 384), (1536, 512), (512, 512), (512, 1024),
         (512, 512)],
        True,
        far=6,
    )(
        tree_order, features, gain_leaf, w_qkv, w_out_leaf, gain_coarse, cotangent,
        w_one, w_two, w_three, w_query, w_keyval, w_out,
    )
    message, root_rows = call(
        message_kernel, [(N_LEAF, 24, 128), (8, 512)], [(4, 24, 128)], True
    )(group, main, roots, *group_swaps(roots))
    got = lax.all_to_all(message, LEAF, 0, 0, tiled=True)
    message = call(attend_kernel, [(N_LEAF, 24, 128)], (), True)(half, got)[0]
    got = lax.all_to_all(message, LEAF, 0, 0, tiled=True)
    bottleneck, d_queries, d_keyval, d_roots, pack = call(
        unpack_kernel, [(16, 512), (16, 512), (16, 1024), (4, 16, 128), (24, 3072)]
    )(got, rows, root_rows, cotangent)
    swap = lambda v: lax.ppermute(v, "co", [(0, 1), (1, 0)])
    upper = call(upper_kernel, [(512, 1024)], (), True)(core, pack, swap(pack))[0]
    upper, *far = lax.optimization_barrier((upper, *group_swaps(d_roots)))
    upper = lax.all_to_all(upper.reshape(64, 8, 1024), CHIPS, 0, 0, tiled=True)
    output, keep, send = call(
        backward_kernel,
        [(16, 512), (64, 88, 128), (64, 88, 128)],
        [(4, 16, 128), (3, 64, 128), (1024, 384), (1024, 128)],
        True,
        pl.CostEstimate(flops=12_000_000_000, bytes_accessed=20_000_000, transcendentals=0),
    )(
        group, d_roots, *far, bottleneck, w_out, d_queries, d_keyval, rows, coarse, cotangent,
        gain_coarse, w_query, w_keyval, w_three, w_two, w_one, w_out_leaf, w_qkv, gain_leaf,
        *saved,
    )
    send, upper = lax.optimization_barrier((send, upper))
    upper = spread(jnp.sum(upper, axis=0), CHIPS, 64).reshape(512, 1024)
    late, upper = lax.optimization_barrier((keep + swap(send), upper))
    late = jnp.sum(lax.all_to_all(late, CHIPS, 0, 0, tiled=True), axis=0)
    late = spread(late, CHIPS, 64)
    upper = call(assemble_upper_kernel, [(512, 512), (512, 1024), (512, 512)], (), True)(
        core, upper, swap(upper)
    )
    late, *upper = lax.optimization_barrier((late, *upper))
    gain_leaf, gain_coarse, *rest = call(
        assemble_kernel,
        [(128,), (512,), (128, 384), (128, 128), (512, 256), (1024, 384), (1536, 512)],
        [(64, 88, 128), (64, 88, 128)],
        True,
        far=2,
        copies=8,
    )(core, late, swap(late))
    return (output, gain_leaf, *rest, gain_coarse, *upper)


def solution(mesh):
    fine = Mesh(mesh.devices.reshape(2, 2, 2, 4, 4), ALL)
    cut = P(ALL, None)
    return jax.shard_map(
        shards,
        mesh=fine,
        in_specs=(cut, cut) + (P(),) * 10 + (cut,),
        out_specs=(cut,) + (P(),) * 10,
        check_vma=False,
    )
```

```python
import jax
import jax.numpy as jnp
from jax import lax
from jax.experimental import pallas as pl
from jax.experimental.pallas import tpu as pltpu
from jax.sharding import Mesh
from jax.sharding import PartitionSpec as P

GRP = ("zh", "co")
LEAF = ("zl", "y", "x")
ALL = GRP + LEAF
CHIPS = ("zh",) + LEAF
N_LEAF = 32
HEADS = 16
SCALE = 32 ** (-0.5)
F32 = jnp.float32


def split(value):
    high = value.astype(jnp.bfloat16)
    return high, (value - high.astype(F32)).astype(jnp.bfloat16)


def dot3(left, right, dims):
    left_high, left_low = split(left)
    right_high, right_low = split(right)
    go = lambda a, b: lax.dot_general(a, b, (dims, ((), ())), preferred_element_type=F32)
    return go(left_high, right_high) + (go(left_high, right_low) + go(left_low, right_high))


def mm(left, right):
    return dot3(left, right, ((1,), (0,)))


def mm_t(left, right):
    return dot3(left, right, ((1,), (1,)))


def t_mm(left, right):
    return dot3(left, right, ((0,), (0,)))


def full(left, right, dims):
    return lax.dot_general(
        left, right, (dims, ((), ())), precision=lax.Precision.HIGHEST, preferred_element_type=F32
    )


def mm6(left, right):
    return full(left, right, ((1,), (0,)))


def mm6_t(left, right):
    return full(left, right, ((1,), (1,)))


def t_mm6(left, right):
    return full(left, right, ((0,), (0,)))


def lanes(at):
    lane = lax.broadcasted_iota(jnp.int32, (1, 128), 1)
    return ((lane >= 32 * at) & (lane < 32 * at + 32)).astype(F32)


def turn(value, by):
    by = by % 128
    return value if by == 0 else pltpu.roll(value, by, 1)


def inverse_rms(values):
    return lax.rsqrt(jnp.mean(values * values, axis=-1, keepdims=True) + 1e-06)


def sigmoid(pre):
    return 1.0 / (1.0 + jnp.exp(-pre))


def softmax(scores):
    weights = jnp.exp(scores - jnp.max(scores, axis=-1, keepdims=True))
    return weights / jnp.sum(weights, axis=-1, keepdims=True)


def four(value):
    return jnp.concatenate([value * lanes(h) for h in range(4)], axis=0)


def slot_one(rows, at):
    return rows.reshape(8, 4, 32, rows.shape[-1])[:, at].reshape(256, rows.shape[-1])


def slot_two(rows, at):
    return rows.reshape(8, 4, 8, rows.shape[-1])[:, at].reshape(64, rows.shape[-1])


def stride_get(ref, at, stride):
    blocks = [ref[j, pl.ds(at, 8, stride=stride), :] for j in range(ref.shape[0])]
    return jnp.concatenate(blocks, axis=1)


def stride_put(ref, at, stride, value):
    for j in range(ref.shape[0]):
        ref[j, pl.ds(at, 8, stride=stride), :] = value[:, 128 * j : 128 * j + 128]


def put_blocks(ref, value):
    for j in range(ref.shape[0]):
        ref[j] = value[:, 128 * j : 128 * j + 128]


def get_blocks(ref):
    return jnp.concatenate([ref[j] for j in range(ref.shape[0])], axis=1)


def slot_three(ref, at):
    return jnp.concatenate([stride_get(ref, 2 * at + a, 8) for a in range(2)], axis=0)


def forward_kernel(
    order, features, gain_leaf, w_qkv, w_out_leaf, gain_coarse, cotangent,
    far_one, far_two, far_three, far_query, far_keyval, far_out,
    unit, packed, weights, attended, mixed, pre_one, pre_two, two, coarse, rows, message, roots,
    ordered, natural, w_one, w_two, w_three, w_query, w_keyval, w_out, arrived,
):
    pairs = (
        (far_one, w_one), (far_two, w_two), (far_three, w_three),
        (far_query, w_query), (far_keyval, w_keyval), (far_out, w_out),
    )
    copies = [pltpu.make_async_copy(*pair, arrived.at[i]) for i, pair in enumerate(pairs)]
    for copy in copies:
        copy.start()
    wait = lambda i: copies[i].wait()

    def fetch(step, carry):
        ball, rest = step // 16, step % 16
        base = ball * 128 + (rest % 4) * 4 + rest // 4
        for d2 in range(4):
            for a in range(2):
                source = order[0, base + 64 * a + 16 * d2]
                ordered[pl.ds(step * 8 + 2 * d2 + a, 1), :] = features[pl.ds(source, 1), :]
        return carry

    lax.fori_loop(0, 128, fetch, 0, unroll=8)
    unit[...] = ordered[...] * inverse_rms(ordered[...])
    packed[...] = mm6(unit[...] * gain_leaf[...], w_qkv[...])

    def ball(step, carry):
        at = pl.ds(step * 128, 128)
        values = packed[at, 256:]
        scores = mm_t(four(packed[at, :128] * SCALE), packed[at, 128:256])
        probs = softmax(scores)
        weights[pl.ds(step * 512, 512), :] = probs
        wide = jnp.concatenate([probs[128 * h : 128 * h + 128] for h in range(4)], axis=1)
        attended[at, :] = mm(wide, four(values))
        return carry

    lax.fori_loop(0, 8, ball, 0, unroll=8)
    joined = ordered[...] + mm6(attended[...], w_out_leaf[...])
    mixed[...] = joined
    wait(0)
    pre = mm6(jnp.concatenate([slot_one(joined, d) for d in range(4)], axis=1), w_one[...])
    pre_one[...] = pre
    one = pre * sigmoid(pre)
    wait(1)
    pre = mm6(jnp.concatenate([slot_two(one, d) for d in range(4)], axis=1), w_two[...])
    pre_two[...] = pre
    put_blocks(two, pre * sigmoid(pre))
    wait(2)
    top = mm6(jnp.concatenate([slot_three(two, d) for d in range(4)], axis=1), w_three[...])
    for a in range(2):
        stride_put(natural, a, 2, top[8 * a : 8 * a + 8])
    top = get_blocks(natural)
    coarse[...] = top
    means = jnp.concatenate(
        [jnp.mean(top[8 * r : 8 * r + 8], axis=0, keepdims=True) for r in range(2)]
        + [jnp.zeros((6, 512), F32)],
        axis=0,
    )
    normed = jnp.concatenate([top * inverse_rms(top), means * inverse_rms(means)], axis=0)
    normed = normed * gain_coarse[...]
    rows[...] = normed
    for i in range(3, 6):
        wait(i)
    queries = mm6(normed[:16], w_query[...])
    keyval = mm6(normed, w_keyval[...])
    d_bottleneck = mm6_t(cotangent[...], w_out[...])
    parts = (queries, keyval[:16, :512], keyval[:16, 512:], d_bottleneck)
    for h in range(HEADS):
        block = slice(128 * (h // 4), 128 * (h // 4) + 128)
        message[h] = sum(
            turn(part[:, block], 32 * (c - h % 4)) * lanes(c) for c, part in enumerate(parts)
        )
    for j in range(8):
        roots[2 * j : 2 * j + 2, :] = keyval[16:18, 128 * j : 128 * j + 128]
    for j in range(4):
        roots[16 + 2 * j : 18 + 2 * j, :] = normed[16:18, 128 * j : 128 * j + 128]


def message_kernel(group, main, roots, one, two, three, message, root_rows, sorted_roots):
    for k, part in enumerate((roots, one, two, three)):
        sorted_roots[group[0] ^ k] = part[...]
    roots = sorted_roots
    block = lambda j: roots[:, 2 * j : 2 * j + 2, :].reshape(8, 128)
    for h in range(HEADS):
        side = turn(block(h // 4), -32 * (h % 4)) * lanes(0)
        side = side + turn(block(4 + h // 4), 32 - 32 * (h % 4)) * lanes(1)
        for half in range(2):
            message[2 * h + half, :16, :] = main[h]
            message[2 * h + half, 16:, :] = side
    for j in range(4):
        root_rows[:, 128 * j : 128 * j + 128] = block(8 + j)


def attend_kernel(half, got, message):
    at = pl.multiple_of(half[0] * 8, 8)
    mine = got[:, pl.ds(at, 8), :].reshape(256, 128)
    every = got[:, :16, :].reshape(512, 128)
    away = got[:, 16:, :].reshape(256, 128)
    queries = mine * lanes(0) * SCALE
    d_out = mine * lanes(3)

    def scores_of(keys, values):
        probs = softmax(mm6_t(queries, keys))
        d_probs = mm6_t(d_out, values)
        d_scores = probs * (d_probs - jnp.sum(probs * d_probs, axis=-1, keepdims=True))
        return probs, d_scores * SCALE

    probs, d_scores = scores_of(turn(every, -32), turn(every, 32))
    front = mm(probs, turn(every, -64) * lanes(0)) + mm(d_scores, every * lanes(1))
    back = t_mm(d_scores, turn(mine, 64) * lanes(2)) + t_mm(probs, d_out)
    probs, d_scores = scores_of(away, turn(away, 64))
    front = front + mm(probs, turn(away, -32) * lanes(0))
    front = front + mm(d_scores, turn(away, 32) * lanes(1))
    side = t_mm(d_scores, mine * lanes(0)) + t_mm(probs, turn(mine, 64) * lanes(1))
    message[:, :16, :] = back.reshape(N_LEAF, 16, 128)
    message[:, pl.ds(at, 8), :] = message[:, pl.ds(at, 8), :] + front.reshape(N_LEAF, 8, 128)
    message[:, 16:, :] = side.reshape(N_LEAF, 8, 128)


def unpack_kernel(got, rows, root_rows, cotangent, bottleneck, d_queries, d_keyval, d_roots, pack):
    pack[16:, :1024] = jnp.zeros((8, 1024), F32)
    pack[16:, 2560:] = jnp.zeros((8, 512), F32)
    pack[:16, 2048:2560] = rows[:16, :]
    pack[16:, 2048:2560] = root_rows[...]
    pack[:16, 2560:] = cotangent[...]
    for block in range(4):
        heads = [got[2 * h] + got[2 * h + 1] for h in range(4 * block, 4 * block + 4)]
        pick = lambda c, rows: sum(
            turn(heads[k][rows], 32 * (k - c)) * lanes(k) for k in range(4)
        )
        own, far = slice(0, 16), slice(16, 24)
        for c, ref in enumerate((bottleneck, d_queries, d_keyval, d_keyval)):
            at = 128 * block + (512 if c == 3 else 0)
            value = pick(c, own)
            ref[:, at : at + 128] = value
            pack[:16, 512 * c + 128 * block : 512 * c + 128 * block + 128] = value
        for c in range(2):
            value = pick(c, far)
            at = 8 * c + 2 * block
            d_roots[:, at : at + 2, :] = value.reshape(4, 2, 128)
            at = 1024 + 512 * c + 128 * block
            pack[16:, at : at + 128] = value


def upper_kernel(core, mine, other, grads):
    both = lambda at, width: jnp.concatenate(
        [mine[:, pl.ds(at, width)], other[:, pl.ds(at, width)]], axis=0
    )
    half = lambda at, width: both(pl.multiple_of(at + core[0] * width, 128), width)
    normed = both(2048, 512)
    grads[:, :256] = t_mm(both(0, 512), half(2560, 256))
    grads[:, 256:512] = t_mm(normed, half(512, 256))
    grads[:, 512:] = t_mm(normed, half(1024, 512))


def assemble_upper_kernel(core, mine, other, grad_query, grad_keyval, grad_out):
    def fill(half, source):
        grad_out[:, 256 * half : 256 * half + 256] = source[:, :256]
        grad_query[:, 256 * half : 256 * half + 256] = source[:, 256:512]
        grad_keyval[:, 512 * half : 512 * half + 512] = source[:, 512:]

    for half in range(2):

        @pl.when(core[0] == half)
        def _():
            fill(half, mine)
            fill(1 - half, other)


def rms_backward(d_normed, values, gain):
    scale = inverse_rms(values)
    unit = values * scale
    d_unit = d_normed * gain
    d_values = scale * (d_unit - unit * jnp.mean(d_unit * unit, axis=-1, keepdims=True))
    return d_values, jnp.sum(d_normed * unit, axis=0, keepdims=True)


def backward_kernel(
    group, d_roots, roots_one, roots_two, roots_three, bottleneck, w_out, d_queries, d_keyval, rows, coarse, cotangent, gain_coarse, w_query, w_keyval,
    w_three, w_two, w_one, w_out_leaf, w_qkv, gain_leaf,
    unit, packed, weights, attended, mixed, pre_one, pre_two, two,
    output, keep, send,
    d_coarse, d_two, d_packed, d_attended,
):
    def put(half, chips, at, value):
        chips, at = pl.ds(*chips), pl.ds(*at)

        @pl.when(core == half)
        def _():
            keep[chips, at, :] = value

        @pl.when(core != half)
        def _():
            send[chips, at, :] = value

    core = group[0] % 2
    output[...] = coarse[...] + mm6(bottleneck[...], w_out[...])
    far = sum(ref[group[0]] for ref in (d_roots, roots_one, roots_two, roots_three))
    far = jnp.concatenate([far[2 * j : 2 * j + 2] for j in range(8)], axis=1)
    d_kv = jnp.concatenate([d_keyval[...], far, jnp.zeros((6, 1024), F32)], axis=0)
    d_rows = mm6_t(d_kv, w_keyval[...])
    top = coarse[...]
    d_top, gain_a = rms_backward(
        d_rows[:16] + mm6_t(d_queries[...], w_query[...]), top, gain_coarse[...]
    )
    means = jnp.concatenate(
        [jnp.mean(top[8 * r : 8 * r + 8], axis=0, keepdims=True) for r in range(2)], axis=0
    )
    d_means, gain_b = rms_backward(d_rows[16:18], means, gain_coarse[...])
    d_means = d_means * 0.125
    d_means = jnp.concatenate(
        [jnp.broadcast_to(d_means[r : r + 1], (8, 512)) for r in range(2)], axis=0
    )
    put_blocks(d_coarse, cotangent[...] + d_top + d_means)
    gain_c = gain_a + gain_b

    d_top = jnp.concatenate([stride_get(d_coarse, a, 2) for a in range(2)], axis=0)
    for d in range(4):
        at = slice(384 * d, 384 * d + 384)
        grad = t_mm(slot_three(two, d), d_top)
        for i in range(4):
            block = grad[:, 128 * i : 128 * i + 128].reshape(16, 24, 128)
            put(i // 2, (16 * d, 16), (24 * (i % 2), 24), block)
        part = mm6_t(d_top, w_three[at, :])
        for a in range(2):
            stride_put(d_two, 2 * d + a, 8, part[8 * a : 8 * a + 8])
    pre = pre_two[...]
    gate = sigmoid(pre)
    d_pre = get_blocks(d_two) * (gate * (1.0 + pre * (1.0 - gate)))
    pre = pre_one[...]
    gate = sigmoid(pre)
    one = pre * gate
    parts = []
    for d in range(4):
        at = slice(256 * d, 256 * d + 256)
        grad = t_mm(slot_two(one, d), d_pre)
        for i in range(3):
            block = grad[:, 128 * i : 128 * i + 128].reshape(32, 8, 128)
            put(d // 2, (32 * (d % 2), 32), (48 + 8 * i, 8), block)
        parts.append(mm_t(d_pre, w_two[at, :]).reshape(8, 1, 8, 256))
    d_one = jnp.concatenate(parts, axis=1).reshape(256, 256)
    d_pre = d_one * (gate * (1.0 + pre * (1.0 - gate)))
    joined = mixed[...]
    parts = []
    for d in range(4):
        at = slice(128 * d, 128 * d + 128)
        grad = t_mm(slot_one(joined, d), d_pre)
        for i in range(2):
            put(i, (16 * d, 16), (72, 8), grad[:, 128 * i : 128 * i + 128].reshape(16, 8, 128))
        parts.append(mm_t(d_pre, w_one[at, :]).reshape(8, 1, 32, 128))
    d_mixed = jnp.concatenate(parts, axis=1).reshape(1024, 128)
    grad_out_leaf = t_mm(attended[...], d_mixed)
    d_attended[...] = mm_t(d_mixed, w_out_leaf[...])

    def ball(step, carry):
        at = pl.ds(step * 128, 128)
        probs = weights[pl.ds(step * 512, 512), :]
        d_out = four(d_attended[at, :])
        d_probs = mm6_t(d_out, packed[at, 256:])
        d_scores = probs * (d_probs - jnp.sum(probs * d_probs, axis=-1, keepdims=True)) * SCALE
        wide = jnp.concatenate([d_scores[128 * h : 128 * h + 128] for h in range(4)], axis=1)
        d_packed[at, :128] = mm(wide, four(packed[at, 128:256]))
        d_packed[at, 128:256] = t_mm(d_scores, four(packed[at, :128]))
        d_packed[at, 256:] = t_mm(probs, d_out)
        return carry

    lax.fori_loop(0, 8, ball, 0, unroll=4)
    grad_qkv = t_mm(unit[...] * gain_leaf[...], d_packed[...])
    blocks = [grad_qkv[:, 128 * i : 128 * i + 128] for i in range(3)] + [grad_out_leaf]
    for i, block in enumerate(blocks):
        put(i // 2, (16 * (i % 2), 16), (80, 8), block.reshape(16, 8, 128))
    d_normed = mm_t(d_packed[...], w_qkv[...])
    gains = jnp.concatenate(
        [jnp.sum(d_normed * unit[...], axis=0, keepdims=True)]
        + [gain_c[:, 128 * j : 128 * j + 128] for j in range(4)]
        + [jnp.zeros((3, 128), F32)],
        axis=0,
    )
    put(0, (32, 1), (80, 8), gains.reshape(1, 8, 128))
    put(0, (33, 31), (80, 8), jnp.zeros((31, 8, 128), F32))
    put(1, (32, 32), (80, 8), jnp.zeros((32, 8, 128), F32))


def place(half, near, outs, staged, left):
    three, two, one = staged
    homes = (
        outs[0].at[:, pl.ds(pl.multiple_of(half * 256, 128), 256)],
        outs[1].at[pl.ds(pl.multiple_of(half * 512, 8), 512), :],
        outs[2].at[:, pl.ds(pl.multiple_of(half * 128, 128), 128)],
    )
    leaving = []
    for i in range(3):
        if i == 0:
            for j in range(2):
                block = near[:, 24 * j : 24 * j + 24, :]
                three[:, 128 * j : 128 * j + 128] = block.reshape(1536, 128)
        elif i == 1:
            for j in range(3):
                block = near[:, 48 + 8 * j : 56 + 8 * j, :]
                two[:, 128 * j : 128 * j + 128] = block.reshape(512, 128)
        else:
            one[...] = near[:, 72:80, :].reshape(512, 128)
        leaving.append(pltpu.make_async_copy(staged[i], homes[i], left.at[i]))
        leaving[-1].start()
    return leaving


def mine_kernel(core, near, three, two, one, stage_a, stage_b, stage_c, left):
    for copy in place(core[0], near, (three, two, one), (stage_a, stage_b, stage_c), left):
        copy.wait()


def other_kernel(
    core, own, near, three_in, two_in, one_in,
    three, two, one, gain_leaf, gain_coarse, grad_qkv, grad_out_leaf,
    stage_a, stage_b, stage_c, left,
):
    del three_in, two_in, one_in
    stages = (stage_a, stage_b, stage_c)
    leaving = place(1 - core[0], near, (three, two, one), stages, left)

    def fill(half, blocks):
        first, second = blocks[0:16].reshape(128, 128), blocks[16:32].reshape(128, 128)
        if half == 0:
            grad_qkv[:, :128] = first
            grad_qkv[:, 128:256] = second
            gain_leaf[...] = blocks[32, 0, :]
            for i in range(4):
                gain_coarse[128 * i : 128 * i + 128] = blocks[32, 1 + i, :]
        else:
            grad_qkv[:, 256:] = first
            grad_out_leaf[...] = second

    for half in range(2):

        @pl.when(core[0] == half)
        def _():
            fill(half, own[:, 80:88, :])
            fill(1 - half, near[:, 80:88, :])

    for copy in leaving:
        copy.wait()


def assemble(core, mine, other):
    pools = [jax.ShapeDtypeStruct(shape, F32) for shape in ((1536, 512), (1024, 384), (512, 256))]
    small = [
        jax.ShapeDtypeStruct(shape, F32) for shape in ((128,), (512,), (128, 384), (128, 128))
    ]
    smem, vmem, hbm = (
        pl.BlockSpec(memory_space=space) for space in (pltpu.SMEM, pltpu.VMEM, pl.ANY)
    )
    rooms = [pltpu.VMEM(shape, F32) for shape in ((1536, 256), (512, 384), (512, 128))]
    rooms.append(pltpu.SemaphoreType.DMA((3,)))
    params = pltpu.CompilerParams(vmem_limit_bytes=24 * 2**20)
    begun = pl.pallas_call(
        mine_kernel,
        out_shape=pools,
        in_specs=[smem, vmem],
        out_specs=[hbm] * 3,
        scratch_shapes=rooms,
        compiler_params=params,
    )(core, mine)
    return pl.pallas_call(
        other_kernel,
        out_shape=pools + small,
        in_specs=[smem, vmem, vmem] + [hbm] * 3,
        out_specs=[hbm] * 3 + [vmem] * 4,
        scratch_shapes=rooms,
        input_output_aliases={3: 0, 4: 1, 5: 2},
        compiler_params=params,
    )(core, mine, other, *begun)


def call(kernel, outs, scratch=(), smem_first=False, cost=None, far=0, limit=56):
    shapes = [jax.ShapeDtypeStruct(shape, F32) for shape in outs]

    rooms = [pltpu.VMEM(shape, F32) for shape in scratch]

    def run(*args):
        specs = [pl.BlockSpec(memory_space=pltpu.VMEM)] * len(args)
        if smem_first:
            specs[0] = pl.BlockSpec(memory_space=pltpu.SMEM)
        if far:
            specs[-far:] = [pl.BlockSpec(memory_space=pl.ANY)] * far
            rooms.append(pltpu.SemaphoreType.DMA((far,)))
        return pl.pallas_call(
            kernel,
            out_shape=shapes,
            in_specs=specs,
            out_specs=[pl.BlockSpec(memory_space=pltpu.VMEM)] * len(shapes),
            scratch_shapes=rooms,
            cost_estimate=cost,
            compiler_params=pltpu.CompilerParams(vmem_limit_bytes=limit * 2**20),
        )(*args)

    return run


def group_swaps(value):
    return [lax.ppermute(value, GRP, [(i, i ^ k) for i in range(4)]) for k in range(1, 4)]


def spread(value, axes, parts):
    wide = jnp.broadcast_to(value[None], (parts,) + value.shape)
    return lax.all_to_all(wide, axes, 0, 0, tiled=True)


def shards(
    features, tree_order, gain_leaf, w_qkv, w_out_leaf, w_one, w_two, w_three, gain_coarse,
    w_query, w_keyval, w_out, cotangent,
):
    half = (lax.axis_index("x") % 2).astype(jnp.int32).reshape(1)
    group = lax.axis_index(GRP).astype(jnp.int32).reshape(1)
    core = lax.axis_index("co").astype(jnp.int32).reshape(1)
    gain_leaf = gain_leaf.reshape(1, 128)
    gain_coarse = gain_coarse.reshape(1, 512)
    saved_shapes = [
        (1024, 128), (1024, 384), (4096, 128), (1024, 128), (1024, 128), (256, 256), (64, 384),
        (3, 64, 128),
    ]
    *saved, coarse, rows, main, roots = call(
        forward_kernel,
        saved_shapes + [(16, 512), (24, 512), (HEADS, 16, 128), (24, 128)],
        [(1024, 128), (4, 16, 128), (512, 256), (1024, 384), (1536, 512), (512, 512), (512, 1024),
         (512, 512)],
        True,
        far=6,
    )(
        tree_order, features, gain_leaf, w_qkv, w_out_leaf, gain_coarse, cotangent,
        w_one, w_two, w_three, w_query, w_keyval, w_out,
    )
    message, root_rows = call(
        message_kernel, [(N_LEAF, 24, 128), (8, 512)], [(4, 24, 128)], True, limit=16
    )(group, main, roots, *group_swaps(roots))
    got = lax.all_to_all(message, LEAF, 0, 0, tiled=True)
    message = call(attend_kernel, [(N_LEAF, 24, 128)], (), True, limit=16)(half, got)[0]
    got = lax.all_to_all(message, LEAF, 0, 0, tiled=True)
    bottleneck, d_queries, d_keyval, d_roots, pack = call(
        unpack_kernel, [(16, 512), (16, 512), (16, 1024), (4, 16, 128), (24, 3072)]
    )(got, rows, root_rows, cotangent)
    swap = lambda v: lax.ppermute(v, "co", [(0, 1), (1, 0)])
    upper = call(upper_kernel, [(512, 1024)], (), True, limit=16)(core, pack, swap(pack))[0]
    upper, *far = lax.optimization_barrier((upper, *group_swaps(d_roots)))
    upper = lax.all_to_all(upper.reshape(64, 8, 1024), CHIPS, 0, 0, tiled=True)
    output, keep, send = call(
        backward_kernel,
        [(16, 512), (64, 88, 128), (64, 88, 128)],
        [(4, 16, 128), (3, 64, 128), (1024, 384), (1024, 128)],
        True,
        pl.CostEstimate(flops=12_000_000_000, bytes_accessed=20_000_000, transcendentals=0),
    )(
        group, d_roots, *far, bottleneck, w_out, d_queries, d_keyval, rows, coarse, cotangent,
        gain_coarse, w_query, w_keyval, w_three, w_two, w_one, w_out_leaf, w_qkv, gain_leaf,
        *saved,
    )
    send, upper = lax.optimization_barrier((send, upper))
    upper = spread(jnp.sum(upper, axis=0), CHIPS, 64).reshape(512, 1024)
    late, upper = lax.optimization_barrier((keep + swap(send), upper))
    late = jnp.sum(lax.all_to_all(late, CHIPS, 0, 0, tiled=True), axis=0)
    late = spread(late, CHIPS, 64)
    upper = call(assemble_upper_kernel, [(512, 512), (512, 1024), (512, 512)], (), True)(
        core, upper, swap(upper)
    )
    late, *upper = lax.optimization_barrier((late, *upper))
    three, two, one, gain_leaf, gain_coarse, grad_qkv, grad_out_leaf = assemble(
        core, late, swap(late)
    )
    return (
        output, gain_leaf, grad_qkv, grad_out_leaf, one, two, three, gain_coarse, *upper,
    )


def solution(mesh):
    fine = Mesh(mesh.devices.reshape(2, 2, 2, 4, 4), ALL)
    cut = P(ALL, None)
    return jax.shard_map(
        shards,
        mesh=fine,
        in_specs=(cut, cut) + (P(),) * 10 + (cut,),
        out_specs=(cut,) + (P(),) * 10,
        check_vma=False,
    )
```

```python
import jax
import jax.numpy as jnp
from jax import lax
from jax.experimental import pallas as pl
from jax.experimental.pallas import tpu as pltpu
from jax.sharding import Mesh
from jax.sharding import PartitionSpec as P

GRP = ("zh", "co")
LEAF = ("zl", "y", "x")
ALL = GRP + LEAF
CHIPS = ("zh",) + LEAF
N_LEAF = 32
HEADS = 16
SCALE = 32 ** (-0.5)
F32 = jnp.float32


def split(value):
    high = value.astype(jnp.bfloat16)
    return high, (value - high.astype(F32)).astype(jnp.bfloat16)


def dot3(left, right, dims):
    left_high, left_low = split(left)
    right_high, right_low = split(right)
    go = lambda a, b: lax.dot_general(a, b, (dims, ((), ())), preferred_element_type=F32)
    return go(left_high, right_high) + (go(left_high, right_low) + go(left_low, right_high))


def mm(left, right):
    return dot3(left, right, ((1,), (0,)))


def mm_t(left, right):
    return dot3(left, right, ((1,), (1,)))


def t_mm(left, right):
    return dot3(left, right, ((0,), (0,)))


def full(left, right, dims):
    return lax.dot_general(
        left, right, (dims, ((), ())), precision=lax.Precision.HIGHEST, preferred_element_type=F32
    )


def mm6(left, right):
    return full(left, right, ((1,), (0,)))


def mm6_t(left, right):
    return full(left, right, ((1,), (1,)))


def t_mm6(left, right):
    return full(left, right, ((0,), (0,)))


def lanes(at):
    lane = lax.broadcasted_iota(jnp.int32, (1, 128), 1)
    return ((lane >= 32 * at) & (lane < 32 * at + 32)).astype(F32)


def turn(value, by):
    by = by % 128
    return value if by == 0 else pltpu.roll(value, by, 1)


def inverse_rms(values):
    return lax.rsqrt(jnp.mean(values * values, axis=-1, keepdims=True) + 1e-06)


def sigmoid(pre):
    return 1.0 / (1.0 + jnp.exp(-pre))


def softmax(scores):
    weights = jnp.exp(scores - jnp.max(scores, axis=-1, keepdims=True))
    return weights / jnp.sum(weights, axis=-1, keepdims=True)


def four(value):
    return jnp.concatenate([value * lanes(h) for h in range(4)], axis=0)


def slot_one(rows, at):
    return rows.reshape(8, 4, 32, rows.shape[-1])[:, at].reshape(256, rows.shape[-1])


def slot_two(rows, at):
    return rows.reshape(8, 4, 8, rows.shape[-1])[:, at].reshape(64, rows.shape[-1])


def stride_get(ref, at, stride):
    blocks = [ref[j, pl.ds(at, 8, stride=stride), :] for j in range(ref.shape[0])]
    return jnp.concatenate(blocks, axis=1)


def stride_put(ref, at, stride, value):
    for j in range(ref.shape[0]):
        ref[j, pl.ds(at, 8, stride=stride), :] = value[:, 128 * j : 128 * j + 128]


def put_blocks(ref, value):
    for j in range(ref.shape[0]):
        ref[j] = value[:, 128 * j : 128 * j + 128]


def get_blocks(ref):
    return jnp.concatenate([ref[j] for j in range(ref.shape[0])], axis=1)


def slot_three(ref, at):
    return jnp.concatenate([stride_get(ref, 2 * at + a, 8) for a in range(2)], axis=0)


def forward_kernel(
    order, features, gain_leaf, w_qkv, w_out_leaf, gain_coarse, cotangent,
    far_one, far_two, far_three, far_query, far_keyval, far_out,
    unit, packed, weights, attended, mixed, pre_one, pre_two, two, coarse, rows, message, roots,
    ordered, natural, w_one, w_two, w_three, w_query, w_keyval, w_out, arrived,
):
    pairs = (
        (far_one, w_one), (far_two, w_two), (far_three, w_three),
        (far_query, w_query), (far_keyval, w_keyval), (far_out, w_out),
    )
    copies = [pltpu.make_async_copy(*pair, arrived.at[i]) for i, pair in enumerate(pairs)]
    for copy in copies:
        copy.start()
    wait = lambda i: copies[i].wait()

    def fetch(step, carry):
        ball, rest = step // 16, step % 16
        base = ball * 128 + (rest % 4) * 4 + rest // 4
        for d2 in range(4):
            for a in range(2):
                source = order[0, base + 64 * a + 16 * d2]
                ordered[pl.ds(step * 8 + 2 * d2 + a, 1), :] = features[pl.ds(source, 1), :]
        return carry

    lax.fori_loop(0, 128, fetch, 0, unroll=8)
    unit[...] = ordered[...] * inverse_rms(ordered[...])
    packed[...] = mm6(unit[...] * gain_leaf[...], w_qkv[...])

    def ball(step, carry):
        at = pl.ds(step * 128, 128)
        values = packed[at, 256:]
        scores = mm_t(four(packed[at, :128] * SCALE), packed[at, 128:256])
        probs = softmax(scores)
        weights[pl.ds(step * 512, 512), :] = probs
        wide = jnp.concatenate([probs[128 * h : 128 * h + 128] for h in range(4)], axis=1)
        attended[at, :] = mm(wide, four(values))
        return carry

    lax.fori_loop(0, 8, ball, 0, unroll=8)
    joined = ordered[...] + mm6(attended[...], w_out_leaf[...])
    mixed[...] = joined
    wait(0)
    pre = mm6(jnp.concatenate([slot_one(joined, d) for d in range(4)], axis=1), w_one[...])
    pre_one[...] = pre
    one = pre * sigmoid(pre)
    wait(1)
    pre = mm6(jnp.concatenate([slot_two(one, d) for d in range(4)], axis=1), w_two[...])
    pre_two[...] = pre
    put_blocks(two, pre * sigmoid(pre))
    wait(2)
    top = mm6(jnp.concatenate([slot_three(two, d) for d in range(4)], axis=1), w_three[...])
    for a in range(2):
        stride_put(natural, a, 2, top[8 * a : 8 * a + 8])
    top = get_blocks(natural)
    coarse[...] = top
    means = jnp.concatenate(
        [jnp.mean(top[8 * r : 8 * r + 8], axis=0, keepdims=True) for r in range(2)]
        + [jnp.zeros((6, 512), F32)],
        axis=0,
    )
    normed = jnp.concatenate([top * inverse_rms(top), means * inverse_rms(means)], axis=0)
    normed = normed * gain_coarse[...]
    rows[...] = normed
    for i in range(3, 6):
        wait(i)
    queries = mm6(normed[:16], w_query[...])
    keyval = mm6(normed, w_keyval[...])
    d_bottleneck = mm6_t(cotangent[...], w_out[...])
    parts = (queries, keyval[:16, :512], keyval[:16, 512:], d_bottleneck)
    for h in range(HEADS):
        block = slice(128 * (h // 4), 128 * (h // 4) + 128)
        message[h] = sum(
            turn(part[:, block], 32 * (c - h % 4)) * lanes(c) for c, part in enumerate(parts)
        )
    for j in range(8):
        roots[2 * j : 2 * j + 2, :] = keyval[16:18, 128 * j : 128 * j + 128]
    for j in range(4):
        roots[16 + 2 * j : 18 + 2 * j, :] = normed[16:18, 128 * j : 128 * j + 128]


def message_kernel(group, main, roots, one, two, three, message, root_rows, sorted_roots):
    for k, part in enumerate((roots, one, two, three)):
        sorted_roots[group[0] ^ k] = part[...]
    roots = sorted_roots
    block = lambda j: roots[:, 2 * j : 2 * j + 2, :].reshape(8, 128)
    for h in range(HEADS):
        side = turn(block(h // 4), -32 * (h % 4)) * lanes(0)
        side = side + turn(block(4 + h // 4), 32 - 32 * (h % 4)) * lanes(1)
        for half in range(2):
            message[2 * h + half, :16, :] = main[h]
            message[2 * h + half, 16:, :] = side
    for j in range(4):
        root_rows[:, 128 * j : 128 * j + 128] = block(8 + j)


def attend_kernel(half, got, message):
    at = pl.multiple_of(half[0] * 8, 8)
    mine = got[:, pl.ds(at, 8), :].reshape(256, 128)
    every = got[:, :16, :].reshape(512, 128)
    away = got[:, 16:, :].reshape(256, 128)
    queries = mine * lanes(0) * SCALE
    d_out = mine * lanes(3)

    def scores_of(keys, values):
        probs = softmax(mm6_t(queries, keys))
        d_probs = mm6_t(d_out, values)
        d_scores = probs * (d_probs - jnp.sum(probs * d_probs, axis=-1, keepdims=True))
        return probs, d_scores * SCALE

    probs, d_scores = scores_of(turn(every, -32), turn(every, 32))
    front = mm(probs, turn(every, -64) * lanes(0)) + mm(d_scores, every * lanes(1))
    back = t_mm(d_scores, turn(mine, 64) * lanes(2)) + t_mm(probs, d_out)
    probs, d_scores = scores_of(away, turn(away, 64))
    front = front + mm(probs, turn(away, -32) * lanes(0))
    front = front + mm(d_scores, turn(away, 32) * lanes(1))
    side = t_mm(d_scores, mine * lanes(0)) + t_mm(probs, turn(mine, 64) * lanes(1))
    message[:, :16, :] = back.reshape(N_LEAF, 16, 128)
    message[:, pl.ds(at, 8), :] = message[:, pl.ds(at, 8), :] + front.reshape(N_LEAF, 8, 128)
    message[:, 16:, :] = side.reshape(N_LEAF, 8, 128)


def unpack_kernel(got, rows, root_rows, cotangent, bottleneck, d_queries, d_keyval, d_roots, pack):
    pack[16:, :1024] = jnp.zeros((8, 1024), F32)
    pack[16:, 2560:] = jnp.zeros((8, 512), F32)
    pack[:16, 2048:2560] = rows[:16, :]
    pack[16:, 2048:2560] = root_rows[...]
    pack[:16, 2560:] = cotangent[...]
    for block in range(4):
        heads = [got[2 * h] + got[2 * h + 1] for h in range(4 * block, 4 * block + 4)]
        pick = lambda c, rows: sum(
            turn(heads[k][rows], 32 * (k - c)) * lanes(k) for k in range(4)
        )
        own, far = slice(0, 16), slice(16, 24)
        for c, ref in enumerate((bottleneck, d_queries, d_keyval, d_keyval)):
            at = 128 * block + (512 if c == 3 else 0)
            value = pick(c, own)
            ref[:, at : at + 128] = value
            pack[:16, 512 * c + 128 * block : 512 * c + 128 * block + 128] = value
        for c in range(2):
            value = pick(c, far)
            at = 8 * c + 2 * block
            d_roots[:, at : at + 2, :] = value.reshape(4, 2, 128)
            at = 1024 + 512 * c + 128 * block
            pack[16:, at : at + 128] = value


def upper_kernel(core, mine, other, grads):
    both = lambda at, width: jnp.concatenate(
        [mine[:, pl.ds(at, width)], other[:, pl.ds(at, width)]], axis=0
    )
    half = lambda at, width: both(pl.multiple_of(at + core[0] * width, 128), width)
    normed = both(2048, 512)
    parts = (
        t_mm(both(0, 512), half(2560, 256)),
        t_mm(normed, half(512, 256)),
        t_mm(normed, half(1024, 512)),
    )
    whole = jnp.concatenate(parts, axis=1)
    for j in range(8):
        block = whole[:, 128 * j : 128 * j + 128].reshape(64, 8, 128)
        grads[:, 8 * j : 8 * j + 8, :] = block


def assemble_upper_kernel(core, mine, other, grad_query, grad_keyval, grad_out):
    def fill(half, source):
        homes = ((grad_out, 256, 0), (grad_query, 256, 2), (grad_keyval, 512, 4))
        for home, width, first in homes:
            for j in range(width // 128):
                at, rows = width * half + 128 * j, 8 * (first + j)
                home[:, at : at + 128] = source[:, rows : rows + 8, :].reshape(512, 128)

    for half in range(2):

        @pl.when(core[0] == half)
        def _():
            fill(half, mine)
            fill(1 - half, other)


def rms_backward(d_normed, values, gain):
    scale = inverse_rms(values)
    unit = values * scale
    d_unit = d_normed * gain
    d_values = scale * (d_unit - unit * jnp.mean(d_unit * unit, axis=-1, keepdims=True))
    return d_values, jnp.sum(d_normed * unit, axis=0, keepdims=True)


def backward_kernel(
    group, d_roots, roots_one, roots_two, roots_three, bottleneck, w_out, d_queries, d_keyval, rows, coarse, cotangent, gain_coarse, w_query, w_keyval,
    w_three, w_two, w_one, w_out_leaf, w_qkv, gain_leaf,
    unit, packed, weights, attended, mixed, pre_one, pre_two, two,
    output, keep, send,
    d_coarse, d_two, d_packed, d_attended,
):
    def put(half, chips, at, value):
        chips, at = pl.ds(*chips), pl.ds(*at)

        @pl.when(core == half)
        def _():
            keep[chips, at, :] = value

        @pl.when(core != half)
        def _():
            send[chips, at, :] = value

    core = group[0] % 2
    output[...] = coarse[...] + mm6(bottleneck[...], w_out[...])
    far = sum(ref[group[0]] for ref in (d_roots, roots_one, roots_two, roots_three))
    far = jnp.concatenate([far[2 * j : 2 * j + 2] for j in range(8)], axis=1)
    d_kv = jnp.concatenate([d_keyval[...], far, jnp.zeros((6, 1024), F32)], axis=0)
    d_rows = mm6_t(d_kv, w_keyval[...])
    top = coarse[...]
    d_top, gain_a = rms_backward(
        d_rows[:16] + mm6_t(d_queries[...], w_query[...]), top, gain_coarse[...]
    )
    means = jnp.concatenate(
        [jnp.mean(top[8 * r : 8 * r + 8], axis=0, keepdims=True) for r in range(2)], axis=0
    )
    d_means, gain_b = rms_backward(d_rows[16:18], means, gain_coarse[...])
    d_means = d_means * 0.125
    d_means = jnp.concatenate(
        [jnp.broadcast_to(d_means[r : r + 1], (8, 512)) for r in range(2)], axis=0
    )
    put_blocks(d_coarse, cotangent[...] + d_top + d_means)
    gain_c = gain_a + gain_b

    d_top = jnp.concatenate([stride_get(d_coarse, a, 2) for a in range(2)], axis=0)
    for d in range(4):
        at = slice(384 * d, 384 * d + 384)
        grad = t_mm(slot_three(two, d), d_top)
        for i in range(4):
            block = grad[:, 128 * i : 128 * i + 128].reshape(16, 24, 128)
            put(i // 2, (16 * d, 16), (24 * (i % 2), 24), block)
        part = mm6_t(d_top, w_three[at, :])
        for a in range(2):
            stride_put(d_two, 2 * d + a, 8, part[8 * a : 8 * a + 8])
    pre = pre_two[...]
    gate = sigmoid(pre)
    d_pre = get_blocks(d_two) * (gate * (1.0 + pre * (1.0 - gate)))
    pre = pre_one[...]
    gate = sigmoid(pre)
    one = pre * gate
    parts = []
    for d in range(4):
        at = slice(256 * d, 256 * d + 256)
        grad = t_mm(slot_two(one, d), d_pre)
        for i in range(3):
            block = grad[:, 128 * i : 128 * i + 128].reshape(32, 8, 128)
            put(d // 2, (32 * (d % 2), 32), (48 + 8 * i, 8), block)
        parts.append(mm_t(d_pre, w_two[at, :]).reshape(8, 1, 8, 256))
    d_one = jnp.concatenate(parts, axis=1).reshape(256, 256)
    d_pre = d_one * (gate * (1.0 + pre * (1.0 - gate)))
    joined = mixed[...]
    parts = []
    for d in range(4):
        at = slice(128 * d, 128 * d + 128)
        grad = t_mm(slot_one(joined, d), d_pre)
        for i in range(2):
            put(i, (16 * d, 16), (72, 8), grad[:, 128 * i : 128 * i + 128].reshape(16, 8, 128))
        parts.append(mm_t(d_pre, w_one[at, :]).reshape(8, 1, 32, 128))
    d_mixed = jnp.concatenate(parts, axis=1).reshape(1024, 128)
    grad_out_leaf = t_mm(attended[...], d_mixed)
    d_attended[...] = mm_t(d_mixed, w_out_leaf[...])

    def ball(step, carry):
        at = pl.ds(step * 128, 128)
        probs = weights[pl.ds(step * 512, 512), :]
        d_out = four(d_attended[at, :])
        d_probs = mm6_t(d_out, packed[at, 256:])
        d_scores = probs * (d_probs - jnp.sum(probs * d_probs, axis=-1, keepdims=True)) * SCALE
        wide = jnp.concatenate([d_scores[128 * h : 128 * h + 128] for h in range(4)], axis=1)
        d_packed[at, :128] = mm(wide, four(packed[at, 128:256]))
        d_packed[at, 128:256] = t_mm(d_scores, four(packed[at, :128]))
        d_packed[at, 256:] = t_mm(probs, d_out)
        return carry

    lax.fori_loop(0, 8, ball, 0, unroll=4)
    grad_qkv = t_mm(unit[...] * gain_leaf[...], d_packed[...])
    blocks = [grad_qkv[:, 128 * i : 128 * i + 128] for i in range(3)] + [grad_out_leaf]
    for i, block in enumerate(blocks):
        put(i // 2, (16 * (i % 2), 16), (80, 8), block.reshape(16, 8, 128))
    d_normed = mm_t(d_packed[...], w_qkv[...])
    gains = jnp.concatenate(
        [jnp.sum(d_normed * unit[...], axis=0, keepdims=True)]
        + [gain_c[:, 128 * j : 128 * j + 128] for j in range(4)]
        + [jnp.zeros((3, 128), F32)],
        axis=0,
    )
    put(0, (32, 1), (80, 8), gains.reshape(1, 8, 128))
    put(0, (33, 31), (80, 8), jnp.zeros((31, 8, 128), F32))
    put(1, (32, 32), (80, 8), jnp.zeros((32, 8, 128), F32))


def merge_kernel(upper, keep, other, both):
    both[:, :64, :] = jnp.broadcast_to(upper[...].reshape(1, 64, 128), (64, 64, 128))
    both[:, 64:, :] = keep[...] + other[...]


def place(half, near, outs, staged, left):
    three, two, one = staged
    homes = (
        outs[0].at[:, pl.ds(pl.multiple_of(half * 256, 128), 256)],
        outs[1].at[pl.ds(pl.multiple_of(half * 512, 8), 512), :],
        outs[2].at[:, pl.ds(pl.multiple_of(half * 128, 128), 128)],
    )
    leaving = []
    for i in range(3):
        if i == 0:
            for j in range(2):
                block = near[:, 24 * j : 24 * j + 24, :]
                three[:, 128 * j : 128 * j + 128] = block.reshape(1536, 128)
        elif i == 1:
            for j in range(3):
                block = near[:, 48 + 8 * j : 56 + 8 * j, :]
                two[:, 128 * j : 128 * j + 128] = block.reshape(512, 128)
        else:
            one[...] = near[:, 72:80, :].reshape(512, 128)
        leaving.append(pltpu.make_async_copy(staged[i], homes[i], left.at[i]))
        leaving[-1].start()
    return leaving


def mine_kernel(core, near, three, two, one, stage_a, stage_b, stage_c, left):
    for copy in place(core[0], near, (three, two, one), (stage_a, stage_b, stage_c), left):
        copy.wait()


def other_kernel(
    core, own, near, three_in, two_in, one_in,
    three, two, one, gain_leaf, gain_coarse, grad_qkv, grad_out_leaf,
    stage_a, stage_b, stage_c, left,
):
    del three_in, two_in, one_in
    stages = (stage_a, stage_b, stage_c)
    leaving = place(1 - core[0], near, (three, two, one), stages, left)

    def fill(half, blocks):
        first, second = blocks[0:16].reshape(128, 128), blocks[16:32].reshape(128, 128)
        if half == 0:
            grad_qkv[:, :128] = first
            grad_qkv[:, 128:256] = second
            gain_leaf[...] = blocks[32, 0, :]
            for i in range(4):
                gain_coarse[128 * i : 128 * i + 128] = blocks[32, 1 + i, :]
        else:
            grad_qkv[:, 256:] = first
            grad_out_leaf[...] = second

    for half in range(2):

        @pl.when(core[0] == half)
        def _():
            fill(half, own[:, 80:88, :])
            fill(1 - half, near[:, 80:88, :])

    for copy in leaving:
        copy.wait()


def assemble(core, mine, other):
    pools = [jax.ShapeDtypeStruct(shape, F32) for shape in ((1536, 512), (1024, 384), (512, 256))]
    small = [
        jax.ShapeDtypeStruct(shape, F32) for shape in ((128,), (512,), (128, 384), (128, 128))
    ]
    smem, vmem, hbm = (
        pl.BlockSpec(memory_space=space) for space in (pltpu.SMEM, pltpu.VMEM, pl.ANY)
    )
    rooms = [pltpu.VMEM(shape, F32) for shape in ((1536, 256), (512, 384), (512, 128))]
    rooms.append(pltpu.SemaphoreType.DMA((3,)))
    params = pltpu.CompilerParams(vmem_limit_bytes=24 * 2**20)
    begun = pl.pallas_call(
        mine_kernel,
        out_shape=pools,
        in_specs=[smem, vmem],
        out_specs=[hbm] * 3,
        scratch_shapes=rooms,
        compiler_params=params,
    )(core, mine)
    return pl.pallas_call(
        other_kernel,
        out_shape=pools + small,
        in_specs=[smem, vmem, vmem] + [hbm] * 3,
        out_specs=[hbm] * 3 + [vmem] * 4,
        scratch_shapes=rooms,
        input_output_aliases={3: 0, 4: 1, 5: 2},
        compiler_params=params,
    )(core, mine, other, *begun)


def call(kernel, outs, scratch=(), smem_first=False, cost=None, far=0, limit=56):
    shapes = [jax.ShapeDtypeStruct(shape, F32) for shape in outs]

    rooms = [pltpu.VMEM(shape, F32) for shape in scratch]

    def run(*args):
        specs = [pl.BlockSpec(memory_space=pltpu.VMEM)] * len(args)
        if smem_first:
            specs[0] = pl.BlockSpec(memory_space=pltpu.SMEM)
        if far:
            specs[-far:] = [pl.BlockSpec(memory_space=pl.ANY)] * far
            rooms.append(pltpu.SemaphoreType.DMA((far,)))
        return pl.pallas_call(
            kernel,
            out_shape=shapes,
            in_specs=specs,
            out_specs=[pl.BlockSpec(memory_space=pltpu.VMEM)] * len(shapes),
            scratch_shapes=rooms,
            cost_estimate=cost,
            compiler_params=pltpu.CompilerParams(vmem_limit_bytes=limit * 2**20),
        )(*args)

    return run


def group_swaps(value):
    return [lax.ppermute(value, GRP, [(i, i ^ k) for i in range(4)]) for k in range(1, 4)]


def spread(value, axes, parts):
    wide = jnp.broadcast_to(value[None], (parts,) + value.shape)
    return lax.all_to_all(wide, axes, 0, 0, tiled=True)


def shards(
    features, tree_order, gain_leaf, w_qkv, w_out_leaf, w_one, w_two, w_three, gain_coarse,
    w_query, w_keyval, w_out, cotangent,
):
    half = (lax.axis_index("x") % 2).astype(jnp.int32).reshape(1)
    group = lax.axis_index(GRP).astype(jnp.int32).reshape(1)
    core = lax.axis_index("co").astype(jnp.int32).reshape(1)
    gain_leaf = gain_leaf.reshape(1, 128)
    gain_coarse = gain_coarse.reshape(1, 512)
    saved_shapes = [
        (1024, 128), (1024, 384), (4096, 128), (1024, 128), (1024, 128), (256, 256), (64, 384),
        (3, 64, 128),
    ]
    *saved, coarse, rows, main, roots = call(
        forward_kernel,
        saved_shapes + [(16, 512), (24, 512), (HEADS, 16, 128), (24, 128)],
        [(1024, 128), (4, 16, 128), (512, 256), (1024, 384), (1536, 512), (512, 512), (512, 1024),
         (512, 512)],
        True,
        far=6,
    )(
        tree_order, features, gain_leaf, w_qkv, w_out_leaf, gain_coarse, cotangent,
        w_one, w_two, w_three, w_query, w_keyval, w_out,
    )
    message, root_rows = call(
        message_kernel, [(N_LEAF, 24, 128), (8, 512)], [(4, 24, 128)], True, limit=16
    )(group, main, roots, *group_swaps(roots))
    got = lax.all_to_all(message, LEAF, 0, 0, tiled=True)
    message = call(attend_kernel, [(N_LEAF, 24, 128)], (), True, limit=16)(half, got)[0]
    got = lax.all_to_all(message, LEAF, 0, 0, tiled=True)
    bottleneck, d_queries, d_keyval, d_roots, pack = call(
        unpack_kernel, [(16, 512), (16, 512), (16, 1024), (4, 16, 128), (24, 3072)]
    )(got, rows, root_rows, cotangent)
    swap = lambda v: lax.ppermute(v, "co", [(0, 1), (1, 0)])
    upper = call(upper_kernel, [(64, 64, 128)], (), True, limit=16)(core, pack, swap(pack))[0]
    upper, *far = lax.optimization_barrier((upper, *group_swaps(d_roots)))
    upper = lax.all_to_all(upper, CHIPS, 0, 0, tiled=True)
    output, keep, send = call(
        backward_kernel,
        [(16, 512), (64, 88, 128), (64, 88, 128)],
        [(4, 16, 128), (3, 64, 128), (1024, 384), (1024, 128)],
        True,
        pl.CostEstimate(flops=12_000_000_000, bytes_accessed=20_000_000, transcendentals=0),
    )(
        group, d_roots, *far, bottleneck, w_out, d_queries, d_keyval, rows, coarse, cotangent,
        gain_coarse, w_query, w_keyval, w_three, w_two, w_one, w_out_leaf, w_qkv, gain_leaf,
        *saved,
    )
    send, upper = lax.optimization_barrier((send, upper))
    both = call(merge_kernel, [(64, 152, 128)], limit=24)(
        jnp.sum(upper, axis=0), keep, swap(send)
    )[0]
    both = lax.all_to_all(both, CHIPS, 0, 0, tiled=True)
    upper, late = both[:, :64], jnp.sum(both[:, 64:], axis=0)
    late = spread(late, CHIPS, 64)
    upper = call(assemble_upper_kernel, [(512, 512), (512, 1024), (512, 512)], (), True)(
        core, upper, swap(upper)
    )
    late, *upper = lax.optimization_barrier((late, *upper))
    three, two, one, gain_leaf, gain_coarse, grad_qkv, grad_out_leaf = assemble(
        core, late, swap(late)
    )
    return (
        output, gain_leaf, grad_qkv, grad_out_leaf, one, two, three, gain_coarse, *upper,
    )


def solution(mesh):
    fine = Mesh(mesh.devices.reshape(2, 2, 2, 4, 4), ALL)
    cut = P(ALL, None)
    return jax.shard_map(
        shards,
        mesh=fine,
        in_specs=(cut, cut) + (P(),) * 10 + (cut,),
        out_specs=(cut,) + (P(),) * 10,
        check_vma=False,
    )
```

```python
import jax
import jax.numpy as jnp
from jax import lax
from jax.experimental import pallas as pl
from jax.experimental.pallas import tpu as pltpu
from jax.sharding import Mesh
from jax.sharding import PartitionSpec as P

GRP = ("zh", "co")
LEAF = ("zl", "y", "x")
ALL = GRP + LEAF
CHIPS = ("zh",) + LEAF
N_LEAF = 32
HEADS = 16
SCALE = 32 ** (-0.5)
F32 = jnp.float32


def split(value):
    high = value.astype(jnp.bfloat16)
    return high, (value - high.astype(F32)).astype(jnp.bfloat16)


def dot3(left, right, dims):
    left_high, left_low = split(left)
    right_high, right_low = split(right)
    go = lambda a, b: lax.dot_general(a, b, (dims, ((), ())), preferred_element_type=F32)
    return go(left_high, right_high) + (go(left_high, right_low) + go(left_low, right_high))


def mm(left, right):
    return dot3(left, right, ((1,), (0,)))


def mm_t(left, right):
    return dot3(left, right, ((1,), (1,)))


def t_mm(left, right):
    return dot3(left, right, ((0,), (0,)))


def full(left, right, dims):
    return lax.dot_general(
        left, right, (dims, ((), ())), precision=lax.Precision.HIGHEST, preferred_element_type=F32
    )


def mm6(left, right):
    return full(left, right, ((1,), (0,)))


def mm6_t(left, right):
    return full(left, right, ((1,), (1,)))


def t_mm6(left, right):
    return full(left, right, ((0,), (0,)))


def lanes(at):
    lane = lax.broadcasted_iota(jnp.int32, (1, 128), 1)
    return ((lane >= 32 * at) & (lane < 32 * at + 32)).astype(F32)


def turn(value, by):
    by = by % 128
    return value if by == 0 else pltpu.roll(value, by, 1)


def inverse_rms(values):
    return lax.rsqrt(jnp.mean(values * values, axis=-1, keepdims=True) + 1e-06)


def sigmoid(pre):
    return 1.0 / (1.0 + jnp.exp(-pre))


def softmax(scores):
    weights = jnp.exp(scores - jnp.max(scores, axis=-1, keepdims=True))
    return weights / jnp.sum(weights, axis=-1, keepdims=True)


def four(value):
    return jnp.concatenate([value * lanes(h) for h in range(4)], axis=0)


def slot_one(rows, at):
    return rows.reshape(8, 4, 32, rows.shape[-1])[:, at].reshape(256, rows.shape[-1])


def slot_two(rows, at):
    return rows.reshape(8, 4, 8, rows.shape[-1])[:, at].reshape(64, rows.shape[-1])


def stride_get(ref, at, stride):
    blocks = [ref[j, pl.ds(at, 8, stride=stride), :] for j in range(ref.shape[0])]
    return jnp.concatenate(blocks, axis=1)


def stride_put(ref, at, stride, value):
    for j in range(ref.shape[0]):
        ref[j, pl.ds(at, 8, stride=stride), :] = value[:, 128 * j : 128 * j + 128]


def put_blocks(ref, value):
    for j in range(ref.shape[0]):
        ref[j] = value[:, 128 * j : 128 * j + 128]


def get_blocks(ref):
    return jnp.concatenate([ref[j] for j in range(ref.shape[0])], axis=1)


def slot_three(ref, at):
    return jnp.concatenate([stride_get(ref, 2 * at + a, 8) for a in range(2)], axis=0)


def forward_kernel(
    order, features, gain_leaf, w_qkv, w_out_leaf, gain_coarse, cotangent,
    far_one, far_two, far_three, far_query, far_keyval, far_out,
    unit, packed, weights, attended, mixed, pre_one, pre_two, two, coarse, rows, message, roots,
    ordered, natural, w_one, w_two, w_three, w_query, w_keyval, w_out, arrived,
):
    pairs = (
        (far_one, w_one), (far_two, w_two), (far_three, w_three),
        (far_query, w_query), (far_keyval, w_keyval), (far_out, w_out),
    )
    copies = [pltpu.make_async_copy(*pair, arrived.at[i]) for i, pair in enumerate(pairs)]
    for copy in copies:
        copy.start()
    wait = lambda i: copies[i].wait()

    def fetch(step, carry):
        ball, rest = step // 16, step % 16
        base = ball * 128 + (rest % 4) * 4 + rest // 4
        for d2 in range(4):
            for a in range(2):
                source = order[0, base + 64 * a + 16 * d2]
                ordered[pl.ds(step * 8 + 2 * d2 + a, 1), :] = features[pl.ds(source, 1), :]
        return carry

    lax.fori_loop(0, 128, fetch, 0, unroll=8)
    unit[...] = ordered[...] * inverse_rms(ordered[...])
    packed[...] = mm6(unit[...] * gain_leaf[...], w_qkv[...])

    def ball(step, carry):
        at = pl.ds(step * 128, 128)
        values = packed[at, 256:]
        scores = mm_t(four(packed[at, :128] * SCALE), packed[at, 128:256])
        probs = softmax(scores)
        weights[pl.ds(step * 512, 512), :] = probs
        wide = jnp.concatenate([probs[128 * h : 128 * h + 128] for h in range(4)], axis=1)
        attended[at, :] = mm(wide, four(values))
        return carry

    lax.fori_loop(0, 8, ball, 0, unroll=8)
    joined = ordered[...] + mm6(attended[...], w_out_leaf[...])
    mixed[...] = joined
    wait(0)
    pre = mm6(jnp.concatenate([slot_one(joined, d) for d in range(4)], axis=1), w_one[...])
    pre_one[...] = pre
    one = pre * sigmoid(pre)
    wait(1)
    pre = mm6(jnp.concatenate([slot_two(one, d) for d in range(4)], axis=1), w_two[...])
    pre_two[...] = pre
    put_blocks(two, pre * sigmoid(pre))
    wait(2)
    top = mm6(jnp.concatenate([slot_three(two, d) for d in range(4)], axis=1), w_three[...])
    for a in range(2):
        stride_put(natural, a, 2, top[8 * a : 8 * a + 8])
    top = get_blocks(natural)
    coarse[...] = top
    means = jnp.concatenate(
        [jnp.mean(top[8 * r : 8 * r + 8], axis=0, keepdims=True) for r in range(2)]
        + [jnp.zeros((6, 512), F32)],
        axis=0,
    )
    normed = jnp.concatenate([top * inverse_rms(top), means * inverse_rms(means)], axis=0)
    normed = normed * gain_coarse[...]
    rows[...] = normed
    for i in range(3, 6):
        wait(i)
    queries = mm6(normed[:16], w_query[...])
    keyval = mm6(normed, w_keyval[...])
    d_bottleneck = mm6_t(cotangent[...], w_out[...])
    parts = (queries, keyval[:16, :512], keyval[:16, 512:], d_bottleneck)
    for h in range(HEADS):
        block = slice(128 * (h // 4), 128 * (h // 4) + 128)
        message[h] = sum(
            turn(part[:, block], 32 * (c - h % 4)) * lanes(c) for c, part in enumerate(parts)
        )
    for j in range(8):
        roots[2 * j : 2 * j + 2, :] = keyval[16:18, 128 * j : 128 * j + 128]
    for j in range(4):
        roots[16 + 2 * j : 18 + 2 * j, :] = normed[16:18, 128 * j : 128 * j + 128]


def message_kernel(group, main, roots, one, two, three, message, root_rows, sorted_roots):
    for k, part in enumerate((roots, one, two, three)):
        sorted_roots[group[0] ^ k] = part[...]
    roots = sorted_roots
    block = lambda j: roots[:, 2 * j : 2 * j + 2, :].reshape(8, 128)
    for h in range(HEADS):
        side = turn(block(h // 4), -32 * (h % 4)) * lanes(0)
        side = side + turn(block(4 + h // 4), 32 - 32 * (h % 4)) * lanes(1)
        for half in range(2):
            message[2 * h + half, :16, :] = main[h]
            message[2 * h + half, 16:, :] = side
    for j in range(4):
        root_rows[:, 128 * j : 128 * j + 128] = block(8 + j)


def attend_kernel(half, got, message):
    at = pl.multiple_of(half[0] * 8, 8)
    mine = got[:, pl.ds(at, 8), :].reshape(256, 128)
    every = got[:, :16, :].reshape(512, 128)
    away = got[:, 16:, :].reshape(256, 128)
    queries = mine * lanes(0) * SCALE
    d_out = mine * lanes(3)

    def scores_of(keys, values):
        probs = softmax(mm6_t(queries, keys))
        d_probs = mm6_t(d_out, values)
        d_scores = probs * (d_probs - jnp.sum(probs * d_probs, axis=-1, keepdims=True))
        return probs, d_scores * SCALE

    probs, d_scores = scores_of(turn(every, -32), turn(every, 32))
    front = mm(probs, turn(every, -64) * lanes(0)) + mm(d_scores, every * lanes(1))
    back = t_mm(d_scores, turn(mine, 64) * lanes(2)) + t_mm(probs, d_out)
    probs, d_scores = scores_of(away, turn(away, 64))
    front = front + mm(probs, turn(away, -32) * lanes(0))
    front = front + mm(d_scores, turn(away, 32) * lanes(1))
    side = t_mm(d_scores, mine * lanes(0)) + t_mm(probs, turn(mine, 64) * lanes(1))
    message[:, :16, :] = back.reshape(N_LEAF, 16, 128)
    message[:, pl.ds(at, 8), :] = message[:, pl.ds(at, 8), :] + front.reshape(N_LEAF, 8, 128)
    message[:, 16:, :] = side.reshape(N_LEAF, 8, 128)


def unpack_kernel(got, rows, root_rows, cotangent, bottleneck, d_queries, d_keyval, d_roots, pack):
    pack[16:, :1024] = jnp.zeros((8, 1024), F32)
    pack[16:, 2560:] = jnp.zeros((8, 512), F32)
    pack[:16, 2048:2560] = rows[:16, :]
    pack[16:, 2048:2560] = root_rows[...]
    pack[:16, 2560:] = cotangent[...]
    for block in range(4):
        heads = [got[2 * h] + got[2 * h + 1] for h in range(4 * block, 4 * block + 4)]
        pick = lambda c, rows: sum(
            turn(heads[k][rows], 32 * (k - c)) * lanes(k) for k in range(4)
        )
        own, far = slice(0, 16), slice(16, 24)
        for c, ref in enumerate((bottleneck, d_queries, d_keyval, d_keyval)):
            at = 128 * block + (512 if c == 3 else 0)
            value = pick(c, own)
            ref[:, at : at + 128] = value
            pack[:16, 512 * c + 128 * block : 512 * c + 128 * block + 128] = value
        for c in range(2):
            value = pick(c, far)
            at = 8 * c + 2 * block
            d_roots[:, at : at + 2, :] = value.reshape(4, 2, 128)
            at = 1024 + 512 * c + 128 * block
            pack[16:, at : at + 128] = value


def upper_kernel(core, mine, other, grads):
    both = lambda at, width: jnp.concatenate(
        [mine[:, pl.ds(at, width)], other[:, pl.ds(at, width)]], axis=0
    )
    half = lambda at, width: both(pl.multiple_of(at + core[0] * width, 128), width)
    normed = both(2048, 512)
    parts = (
        t_mm(both(0, 512), half(2560, 256)),
        t_mm(normed, half(512, 256)),
        t_mm(normed, half(1024, 512)),
    )
    whole = jnp.concatenate(parts, axis=1)
    for j in range(8):
        block = whole[:, 128 * j : 128 * j + 128].reshape(64, 8, 128)
        grads[:, 8 * j : 8 * j + 8, :] = block


def assemble_upper_kernel(core, mine, other, grad_query, grad_keyval, grad_out):
    def fill(half, source):
        homes = ((grad_out, 256, 0), (grad_query, 256, 2), (grad_keyval, 512, 4))
        for home, width, first in homes:
            for j in range(width // 128):
                at, rows = width * half + 128 * j, 8 * (first + j)
                home[:, at : at + 128] = source[:, rows : rows + 8, :].reshape(512, 128)

    for half in range(2):

        @pl.when(core[0] == half)
        def _():
            fill(half, mine)
            fill(1 - half, other)


def rms_backward(d_normed, values, gain):
    scale = inverse_rms(values)
    unit = values * scale
    d_unit = d_normed * gain
    d_values = scale * (d_unit - unit * jnp.mean(d_unit * unit, axis=-1, keepdims=True))
    return d_values, jnp.sum(d_normed * unit, axis=0, keepdims=True)


def backward_kernel(
    group, d_roots, roots_one, roots_two, roots_three, bottleneck, w_out, d_queries, d_keyval, rows, coarse, cotangent, gain_coarse, w_query, w_keyval,
    w_three, w_two, w_one, w_out_leaf, w_qkv, gain_leaf,
    unit, packed, weights, attended, mixed, pre_one, pre_two, two,
    output, keep, send,
    d_coarse, d_two, d_packed, d_attended,
):
    def put(half, chips, at, value):
        chips, at = pl.ds(*chips), pl.ds(*at)

        @pl.when(core == half)
        def _():
            keep[chips, at, :] = value

        @pl.when(core != half)
        def _():
            send[chips, at, :] = value

    core = group[0] % 2
    output[...] = coarse[...] + mm6(bottleneck[...], w_out[...])
    far = sum(ref[group[0]] for ref in (d_roots, roots_one, roots_two, roots_three))
    far = jnp.concatenate([far[2 * j : 2 * j + 2] for j in range(8)], axis=1)
    d_kv = jnp.concatenate([d_keyval[...], far, jnp.zeros((6, 1024), F32)], axis=0)
    d_rows = mm6_t(d_kv, w_keyval[...])
    top = coarse[...]
    d_top, gain_a = rms_backward(
        d_rows[:16] + mm6_t(d_queries[...], w_query[...]), top, gain_coarse[...]
    )
    means = jnp.concatenate(
        [jnp.mean(top[8 * r : 8 * r + 8], axis=0, keepdims=True) for r in range(2)], axis=0
    )
    d_means, gain_b = rms_backward(d_rows[16:18], means, gain_coarse[...])
    d_means = d_means * 0.125
    d_means = jnp.concatenate(
        [jnp.broadcast_to(d_means[r : r + 1], (8, 512)) for r in range(2)], axis=0
    )
    put_blocks(d_coarse, cotangent[...] + d_top + d_means)
    gain_c = gain_a + gain_b

    d_top = jnp.concatenate([stride_get(d_coarse, a, 2) for a in range(2)], axis=0)
    for d in range(4):
        at = slice(384 * d, 384 * d + 384)
        grad = t_mm(slot_three(two, d), d_top)
        for i in range(4):
            block = grad[:, 128 * i : 128 * i + 128].reshape(16, 24, 128)
            put(i // 2, (16 * d, 16), (24 * (i % 2), 24), block)
        part = mm6_t(d_top, w_three[at, :])
        for a in range(2):
            stride_put(d_two, 2 * d + a, 8, part[8 * a : 8 * a + 8])
    pre = pre_two[...]
    gate = sigmoid(pre)
    d_pre = get_blocks(d_two) * (gate * (1.0 + pre * (1.0 - gate)))
    pre = pre_one[...]
    gate = sigmoid(pre)
    one = pre * gate
    parts = []
    for d in range(4):
        at = slice(256 * d, 256 * d + 256)
        grad = t_mm(slot_two(one, d), d_pre)
        for i in range(3):
            block = grad[:, 128 * i : 128 * i + 128].reshape(32, 8, 128)
            put(d // 2, (32 * (d % 2), 32), (48 + 8 * i, 8), block)
        parts.append(mm_t(d_pre, w_two[at, :]).reshape(8, 1, 8, 256))
    d_one = jnp.concatenate(parts, axis=1).reshape(256, 256)
    d_pre = d_one * (gate * (1.0 + pre * (1.0 - gate)))
    joined = mixed[...]
    parts = []
    for d in range(4):
        at = slice(128 * d, 128 * d + 128)
        grad = t_mm(slot_one(joined, d), d_pre)
        for i in range(2):
            put(i, (16 * d, 16), (72, 8), grad[:, 128 * i : 128 * i + 128].reshape(16, 8, 128))
        parts.append(mm_t(d_pre, w_one[at, :]).reshape(8, 1, 32, 128))
    d_mixed = jnp.concatenate(parts, axis=1).reshape(1024, 128)
    grad_out_leaf = t_mm(attended[...], d_mixed)
    d_attended[...] = mm_t(d_mixed, w_out_leaf[...])

    def ball(step, carry):
        at = pl.ds(step * 128, 128)
        probs = weights[pl.ds(step * 512, 512), :]
        d_out = four(d_attended[at, :])
        d_probs = mm6_t(d_out, packed[at, 256:])
        d_scores = probs * (d_probs - jnp.sum(probs * d_probs, axis=-1, keepdims=True)) * SCALE
        wide = jnp.concatenate([d_scores[128 * h : 128 * h + 128] for h in range(4)], axis=1)
        d_packed[at, :128] = mm(wide, four(packed[at, 128:256]))
        d_packed[at, 128:256] = t_mm(d_scores, four(packed[at, :128]))
        d_packed[at, 256:] = t_mm(probs, d_out)
        return carry

    lax.fori_loop(0, 8, ball, 0, unroll=4)
    grad_qkv = t_mm(unit[...] * gain_leaf[...], d_packed[...])
    blocks = [grad_qkv[:, 128 * i : 128 * i + 128] for i in range(3)] + [grad_out_leaf]
    for i, block in enumerate(blocks):
        put(i // 2, (16 * (i % 2), 16), (80, 8), block.reshape(16, 8, 128))
    d_normed = mm_t(d_packed[...], w_qkv[...])
    gains = jnp.concatenate(
        [jnp.sum(d_normed * unit[...], axis=0, keepdims=True)]
        + [gain_c[:, 128 * j : 128 * j + 128] for j in range(4)]
        + [jnp.zeros((3, 128), F32)],
        axis=0,
    )
    put(0, (32, 1), (80, 8), gains.reshape(1, 8, 128))
    put(0, (33, 31), (80, 8), jnp.zeros((31, 8, 128), F32))
    put(1, (32, 32), (80, 8), jnp.zeros((32, 8, 128), F32))


def merge_kernel(upper, keep, other, both):
    both[:, :64, :] = jnp.broadcast_to(upper[...].reshape(1, 64, 128), (64, 64, 128))
    both[:, 64:, :] = keep[...] + other[...]


def spread_kernel(both, wide):
    total = jnp.sum(both[:, 64:, :], axis=0, keepdims=True)
    wide[...] = jnp.broadcast_to(total, (64, 88, 128))


def place(half, near, outs, staged, left):
    three, two, one = staged
    homes = (
        outs[0].at[:, pl.ds(pl.multiple_of(half * 256, 128), 256)],
        outs[1].at[pl.ds(pl.multiple_of(half * 512, 8), 512), :],
        outs[2].at[:, pl.ds(pl.multiple_of(half * 128, 128), 128)],
    )
    leaving = []
    for i in range(3):
        if i == 0:
            for j in range(2):
                block = near[:, 24 * j : 24 * j + 24, :]
                three[:, 128 * j : 128 * j + 128] = block.reshape(1536, 128)
        elif i == 1:
            for j in range(3):
                block = near[:, 48 + 8 * j : 56 + 8 * j, :]
                two[:, 128 * j : 128 * j + 128] = block.reshape(512, 128)
        else:
            one[...] = near[:, 72:80, :].reshape(512, 128)
        leaving.append(pltpu.make_async_copy(staged[i], homes[i], left.at[i]))
        leaving[-1].start()
    return leaving


def mine_kernel(core, near, three, two, one, stage_a, stage_b, stage_c, left):
    for copy in place(core[0], near, (three, two, one), (stage_a, stage_b, stage_c), left):
        copy.wait()


def other_kernel(
    core, own, near, three_in, two_in, one_in,
    three, two, one, gain_leaf, gain_coarse, grad_qkv, grad_out_leaf,
    stage_a, stage_b, stage_c, left,
):
    del three_in, two_in, one_in
    stages = (stage_a, stage_b, stage_c)
    leaving = place(1 - core[0], near, (three, two, one), stages, left)

    def fill(half, blocks):
        first, second = blocks[0:16].reshape(128, 128), blocks[16:32].reshape(128, 128)
        if half == 0:
            grad_qkv[:, :128] = first
            grad_qkv[:, 128:256] = second
            gain_leaf[...] = blocks[32, 0, :]
            for i in range(4):
                gain_coarse[128 * i : 128 * i + 128] = blocks[32, 1 + i, :]
        else:
            grad_qkv[:, 256:] = first
            grad_out_leaf[...] = second

    for half in range(2):

        @pl.when(core[0] == half)
        def _():
            fill(half, own[:, 80:88, :])
            fill(1 - half, near[:, 80:88, :])

    for copy in leaving:
        copy.wait()


def assemble(core, mine, other):
    pools = [jax.ShapeDtypeStruct(shape, F32) for shape in ((1536, 512), (1024, 384), (512, 256))]
    small = [
        jax.ShapeDtypeStruct(shape, F32) for shape in ((128,), (512,), (128, 384), (128, 128))
    ]
    smem, vmem, hbm = (
        pl.BlockSpec(memory_space=space) for space in (pltpu.SMEM, pltpu.VMEM, pl.ANY)
    )
    rooms = [pltpu.VMEM(shape, F32) for shape in ((1536, 256), (512, 384), (512, 128))]
    rooms.append(pltpu.SemaphoreType.DMA((3,)))
    params = pltpu.CompilerParams(vmem_limit_bytes=24 * 2**20)
    begun = pl.pallas_call(
        mine_kernel,
        out_shape=pools,
        in_specs=[smem, vmem],
        out_specs=[hbm] * 3,
        scratch_shapes=rooms,
        compiler_params=params,
    )(core, mine)
    return pl.pallas_call(
        other_kernel,
        out_shape=pools + small,
        in_specs=[smem, vmem, vmem] + [hbm] * 3,
        out_specs=[hbm] * 3 + [vmem] * 4,
        scratch_shapes=rooms,
        input_output_aliases={3: 0, 4: 1, 5: 2},
        compiler_params=params,
    )(core, mine, other, *begun)


def call(kernel, outs, scratch=(), smem_first=False, cost=None, far=0, limit=56):
    shapes = [jax.ShapeDtypeStruct(shape, F32) for shape in outs]

    rooms = [pltpu.VMEM(shape, F32) for shape in scratch]

    def run(*args):
        specs = [pl.BlockSpec(memory_space=pltpu.VMEM)] * len(args)
        if smem_first:
            specs[0] = pl.BlockSpec(memory_space=pltpu.SMEM)
        if far:
            specs[-far:] = [pl.BlockSpec(memory_space=pl.ANY)] * far
            rooms.append(pltpu.SemaphoreType.DMA((far,)))
        return pl.pallas_call(
            kernel,
            out_shape=shapes,
            in_specs=specs,
            out_specs=[pl.BlockSpec(memory_space=pltpu.VMEM)] * len(shapes),
            scratch_shapes=rooms,
            cost_estimate=cost,
            compiler_params=pltpu.CompilerParams(vmem_limit_bytes=limit * 2**20),
        )(*args)

    return run


def group_swaps(value):
    return [lax.ppermute(value, GRP, [(i, i ^ k) for i in range(4)]) for k in range(1, 4)]


def shards(
    features, tree_order, gain_leaf, w_qkv, w_out_leaf, w_one, w_two, w_three, gain_coarse,
    w_query, w_keyval, w_out, cotangent,
):
    half = (lax.axis_index("x") % 2).astype(jnp.int32).reshape(1)
    group = lax.axis_index(GRP).astype(jnp.int32).reshape(1)
    core = lax.axis_index("co").astype(jnp.int32).reshape(1)
    gain_leaf = gain_leaf.reshape(1, 128)
    gain_coarse = gain_coarse.reshape(1, 512)
    saved_shapes = [
        (1024, 128), (1024, 384), (4096, 128), (1024, 128), (1024, 128), (256, 256), (64, 384),
        (3, 64, 128),
    ]
    *saved, coarse, rows, main, roots = call(
        forward_kernel,
        saved_shapes + [(16, 512), (24, 512), (HEADS, 16, 128), (24, 128)],
        [(1024, 128), (4, 16, 128), (512, 256), (1024, 384), (1536, 512), (512, 512), (512, 1024),
         (512, 512)],
        True,
        far=6,
    )(
        tree_order, features, gain_leaf, w_qkv, w_out_leaf, gain_coarse, cotangent,
        w_one, w_two, w_three, w_query, w_keyval, w_out,
    )
    message, root_rows = call(
        message_kernel, [(N_LEAF, 24, 128), (8, 512)], [(4, 24, 128)], True, limit=16
    )(group, main, roots, *group_swaps(roots))
    got = lax.all_to_all(message, LEAF, 0, 0, tiled=True)
    message = call(attend_kernel, [(N_LEAF, 24, 128)], (), True, limit=16)(half, got)[0]
    got = lax.all_to_all(message, LEAF, 0, 0, tiled=True)
    bottleneck, d_queries, d_keyval, d_roots, pack = call(
        unpack_kernel, [(16, 512), (16, 512), (16, 1024), (4, 16, 128), (24, 3072)]
    )(got, rows, root_rows, cotangent)
    swap = lambda v: lax.ppermute(v, "co", [(0, 1), (1, 0)])
    upper = call(upper_kernel, [(64, 64, 128)], (), True, limit=16)(core, pack, swap(pack))[0]
    upper, *far = lax.optimization_barrier((upper, *group_swaps(d_roots)))
    upper = lax.all_to_all(upper, CHIPS, 0, 0, tiled=True)
    output, keep, send = call(
        backward_kernel,
        [(16, 512), (64, 88, 128), (64, 88, 128)],
        [(4, 16, 128), (3, 64, 128), (1024, 384), (1024, 128)],
        True,
        pl.CostEstimate(flops=12_000_000_000, bytes_accessed=20_000_000, transcendentals=0),
    )(
        group, d_roots, *far, bottleneck, w_out, d_queries, d_keyval, rows, coarse, cotangent,
        gain_coarse, w_query, w_keyval, w_three, w_two, w_one, w_out_leaf, w_qkv, gain_leaf,
        *saved,
    )
    send, upper = lax.optimization_barrier((send, upper))
    both = call(merge_kernel, [(64, 152, 128)], limit=24)(
        jnp.sum(upper, axis=0), keep, swap(send)
    )[0]
    both = lax.all_to_all(both, CHIPS, 0, 0, tiled=True)
    late = call(spread_kernel, [(64, 88, 128)], limit=24)(both)[0]
    late = lax.all_to_all(late, CHIPS, 0, 0, tiled=True)
    upper = both[:, :64]
    upper = call(assemble_upper_kernel, [(512, 512), (512, 1024), (512, 512)], (), True)(
        core, upper, swap(upper)
    )
    late, *upper = lax.optimization_barrier((late, *upper))
    three, two, one, gain_leaf, gain_coarse, grad_qkv, grad_out_leaf = assemble(
        core, late, swap(late)
    )
    return (
        output, gain_leaf, grad_qkv, grad_out_leaf, one, two, three, gain_coarse, *upper,
    )


def solution(mesh):
    fine = Mesh(mesh.devices.reshape(2, 2, 2, 4, 4), ALL)
    cut = P(ALL, None)
    return jax.shard_map(
        shards,
        mesh=fine,
        in_specs=(cut, cut) + (P(),) * 10 + (cut,),
        out_specs=(cut,) + (P(),) * 10,
        check_vma=False,
    )
```
